256 devices in a mesh: roll: 32 (over y, x, core), tp: 8 (over z).
Axes of the slice: x: 4, y: 4, z: 8, core: 2. Of those that a mesh axis runs over, the one named last changes fastest.
Arguments:
- queries: bfloat16 [4096, 4, 64, 128], P('roll', None, 'tp'), may hold values from -8 to 8
- new_keys: bfloat16 [4096, 4, 8, 128], P('roll', None, 'tp'), may hold values from -6 to 6
- new_values: bfloat16 [4096, 4, 8, 128], P('roll', None, 'tp'), may hold values from -6 to 6
- tail_keys: bfloat16 [4096, 8, 128, 128], P('roll', 'tp'), may hold values from -8 to 8
- tail_values: bfloat16 [4096, 8, 128, 128], P('roll', 'tp'), may hold values from -6 to 6
- prefix_keys: bfloat16 [64, 8, 1024, 128], P('roll', 'tp'), may hold values from -8 to 8
- prefix_values: bfloat16 [64, 8, 1024, 128], P('roll', 'tp'), may hold values from -6 to 6
- route_owner: int32 [32, 128], P('roll', 'tp'), may hold values from 0 to 31, as said below
- group_slot: int32 [32, 128], P('roll', 'tp'), may hold values from 0 to 1
- tail_len: int32 [32, 128], P('roll', 'tp'), may hold values from 1 to 128, 10240 in all within a row
Outputs:
- attended: bfloat16 [4096, 4, 64, 128], P('roll', None, 'tp')
The draws below stay inside these ranges and needn't reach their ends.
Inputs may be any that keep to these rules, and one draw needn't show every extreme that they name: `route_owner`: within one device's rows each owner is named at most 8 times, and one owner, drawn afresh, is named exactly 8 times by the rows of every device.
All inputs are finite; a program needn't handle non-finite values. No bound on the sum of `tail_len` on one device may be relied on, other than what follows from the above.
Results may differ from the reference program's by a relative error of at most 0.0056.
Values may be sent and summed in bfloat16 or wider, within the bound.
No kernel may reach another device: no remote copies, remote signals or barrier semaphores. Data moves between devices by JAX's collectives and lax.ppermute only.
A program may use at most 192 MiB of HBM per device.

```python
import math
import jax
import jax.numpy as jnp
import numpy as np
from jax import lax

QH = 64
KVH = 8
HD = 128
STEPS = 4
ROWS_DEV = 128
TAIL = 128
PREF = 1024
G_DEV = 2
OWNERS = 32
ROWS = 4096
GROUPS = 64
CAP = 8


def draw_queries(key, part):
    key = jax.random.fold_in(key, 101)
    values = jnp.clip(jax.random.normal(key, (ROWS, STEPS, QH, HD), jnp.float32), -6.0, 6.0)
    return values.astype(jnp.bfloat16)


def drawn_keys(key, shape):
    values = jnp.clip(jax.random.normal(key, shape, jnp.float32), -6.0, 6.0)
    return values


def draw_prefix_keys(key, part):
    key = jax.random.fold_in(key, 202)
    return drawn_keys(key, (GROUPS, KVH, PREF, HD)).astype(jnp.bfloat16)


def draw_tail_keys(key, part):
    key = jax.random.fold_in(key, 303)
    return drawn_keys(key, (ROWS, KVH, TAIL, HD)).astype(jnp.bfloat16)


def draw_route_owner(key, part):
    key = jax.random.fold_in(key, 404)
    hot_key, rest_key = jax.random.split(key)
    hot = jax.random.randint(hot_key, (), 0, OWNERS)
    device_keys = jax.random.split(rest_key, OWNERS)

    def one_device(device_key):
        first, second = jax.random.split(device_key)
        slots = jax.random.permutation(first, (OWNERS - 1) * CAP)[:ROWS_DEV - CAP]
        other = (slots // CAP).astype(jnp.int32)
        other = other + (other >= hot).astype(jnp.int32)
        names = jnp.concatenate([jnp.full((CAP,), hot, jnp.int32), other])
        order = jax.random.permutation(second, ROWS_DEV)
        return names[order]
    return jax.vmap(one_device)(device_keys)


def touch_ends(array, stream_key, low, high):
    dims = array.shape
    place = [jax.random.randint(jax.random.fold_in(stream_key, axis), (), 0, dims[axis]) for axis in range(len(dims))]
    array = array.at[tuple(place)].set(low)
    longest = dims.index(max(dims))
    place[longest] = (place[longest] + 1) % dims[longest]
    return array.at[tuple(place)].set(high)


def steps_of(stream_key, extent, cuts, least, high):
    def one(dim, shards_of):
        draws = jax.random.uniform(jax.random.fold_in(jax.random.fold_in(stream_key, 6), dim), (shards_of,), jnp.float32, least / len(cuts), high / len(cuts))
        return jnp.repeat(jnp.exp(draws), extent[dim] // shards_of).reshape((-1,) + (1,) * (len(extent) - dim - 1))

    factor_of = one(*cuts[0])
    for cut in cuts[1:]:
        factor_of = factor_of * one(*cut)
    return factor_of


def length_profile(amount, total, most, skew):
    weights = [(1 << 20) // math.isqrt(standing ** skew) + 1 for standing in range(2, amount + 1)]
    rest, given = total - most - (amount - 1), [1] * (amount - 1)
    while rest > 0:
        candidates = [i for i in range(amount - 1) if given[i] < most]
        mass, left = sum([weights[i] for i in candidates]), rest
        for i in candidates:
            more = min(most - given[i], max(1, left * weights[i] // mass), rest)
            given[i] = given[i] + more
            rest = rest - more
    return np.array([most] + given)


def uneven(key, number_of, total, limit, slope):
    if number_of == 2:
        one = jax.random.randint(key, (), max(1, total - limit), min(limit, total - 1) + 1)
        return jnp.stack([one, total - one])
    sizes = jnp.asarray(length_profile(number_of, total, limit, slope), jnp.int32)
    couples = (number_of - 1) // 2
    donor, receiver = sizes[1:1 + 2 * couples:2], sizes[2:2 + 2 * couples:2]
    margin = jnp.minimum(donor - 1, limit - receiver)
    shifted = jax.random.randint(jax.random.fold_in(key, 1), (couples,), 0, 1 << 20) % (margin + 1)
    sizes = sizes.at[1:1 + 2 * couples:2].set(donor - shifted).at[2:2 + 2 * couples:2].set(receiver + shifted)
    return sizes[jax.random.permutation(jax.random.fold_in(key, 2), number_of)]


def noise(key, dims, deviation, limit, pieces=(), kind=jnp.bfloat16):
    result = deviation * jax.random.normal(key, dims, jnp.float32)
    if pieces:
        result = result * steps_of(key, dims, pieces, -0.22, 0.18)
    return jnp.clip(result, -limit, limit).astype(kind)


def setup_inputs(seed: int = 0) -> dict:
    seeds = jax.random.split(jax.random.key(seed), 11)
    queries = draw_queries(jax.random.fold_in(seeds[10], 71), 0)
    new_keys = noise(seeds[1], (ROWS, STEPS, KVH, HD), 1.0, 6.0, ((0, 32), (2, 8)))
    new_values = noise(seeds[2], (ROWS, STEPS, KVH, HD), 1.0, 6.0, ((0, 32), (2, 8)))
    tail_keys = draw_tail_keys(jax.random.fold_in(seeds[10], 71), 0)
    tail_values = noise(seeds[4], (ROWS, KVH, TAIL, HD), 1.0, 6.0, ((0, 32), (1, 8)))
    prefix_keys = draw_prefix_keys(jax.random.fold_in(seeds[10], 71), 0)
    prefix_values = noise(seeds[6], (GROUPS, KVH, PREF, HD), 1.0, 6.0, ((0, 32), (1, 8)))
    route_owner = draw_route_owner(jax.random.fold_in(seeds[10], 71), 0)
    group_slot = touch_ends(jax.random.randint(seeds[8], (OWNERS, ROWS_DEV), 0, G_DEV), jax.random.fold_in(seeds[8], 1), 0, G_DEV - 1).astype(jnp.int32)
    tail_len = jax.vmap(lambda own: uneven(own, ROWS_DEV, ROWS_DEV * TAIL * 5 // 8, TAIL, 2))(jax.random.split(seeds[9], OWNERS)).reshape((OWNERS, ROWS_DEV)).astype(jnp.int32)
    return dict(queries=queries, new_keys=new_keys, new_values=new_values, tail_keys=tail_keys, tail_values=tail_values, prefix_keys=prefix_keys, prefix_values=prefix_values, route_owner=route_owner, group_slot=group_slot, tail_len=tail_len)


def rounded(values):
    return lax.optimization_barrier(values.astype(jnp.bfloat16)).astype(jnp.float32)

def reference(queries, new_keys, new_values, tail_keys, tail_values, prefix_keys, prefix_values, route_owner, group_slot, tail_len):
    groups = (route_owner * G_DEV + group_slot).reshape(-1).astype(jnp.int32)
    lengths = tail_len.reshape(-1).astype(jnp.int32)
    scale = 1.0 / math.sqrt(HD)
    per_group = QH // KVH

    def one_row(item):
        query, group, length, t_keys, t_values, n_keys, n_values = item
        q_five = query.astype(jnp.float32).reshape(STEPS, KVH, per_group, HD)
        p_keys = lax.dynamic_index_in_dim(prefix_keys, group, 0, keepdims=False).astype(jnp.float32)
        p_values = lax.dynamic_index_in_dim(prefix_values, group, 0, keepdims=False).astype(jnp.float32)
        scores = jnp.einsum('skgd,kjd->skgj', q_five, p_keys) * scale
        top_p = lax.optimization_barrier(jnp.max(scores, axis=-1, keepdims=True))
        expo = jnp.exp(scores - top_p)
        total_p = lax.optimization_barrier(jnp.sum(expo, axis=-1, keepdims=True))
        prefix_part = jnp.einsum('skgj,kjd->skgd', rounded(expo), p_values) / total_p
        prefix_part = rounded(prefix_part)
        lse_p = top_p[..., 0] + jnp.log(total_p[..., 0])
        tail_scores = jnp.einsum('skgd,ktd->skgt', q_five, t_keys.astype(jnp.float32)) * scale
        valid = jnp.arange(TAIL, dtype=jnp.int32) < length
        tail_scores = jnp.where(valid, tail_scores, -jnp.inf)
        new_scores = jnp.einsum('skgd,ukd->skgu', q_five, n_keys.astype(jnp.float32)) * scale
        causal = jnp.arange(STEPS)[None, :] <= jnp.arange(STEPS)[:, None]
        new_scores = jnp.where(causal[:, None, None, :], new_scores, -jnp.inf)
        top_t = jnp.maximum(lax.optimization_barrier(jnp.max(tail_scores, axis=-1, keepdims=True)), lax.optimization_barrier(jnp.max(new_scores, axis=-1, keepdims=True)))
        expo_t = jnp.exp(tail_scores - top_t)
        expo_n = jnp.exp(new_scores - top_t)
        total_t = lax.optimization_barrier(jnp.sum(expo_t, axis=-1, keepdims=True)) + lax.optimization_barrier(jnp.sum(expo_n, axis=-1, keepdims=True))
        tail_part = jnp.einsum('skgt,ktd->skgd', rounded(expo_t), t_values.astype(jnp.float32))
        tail_part = tail_part + jnp.einsum('skgu,ukd->skgd', rounded(expo_n), n_values.astype(jnp.float32))
        tail_part = tail_part / total_t
        lse_t = top_t[..., 0] + jnp.log(total_t[..., 0])
        upper = jnp.maximum(lse_p, lse_t)
        weight_p = jnp.exp(lse_p - upper)
        weight_t = jnp.exp(lse_t - upper)
        merged = (weight_p[..., None] * prefix_part + weight_t[..., None] * tail_part) / (weight_p + weight_t)[..., None]
        return merged.reshape(STEPS, QH, HD).astype(jnp.bfloat16)
    return lax.map(one_row, (queries, groups, lengths, tail_keys, tail_values, new_keys, new_values))
```

```python
import functools
import math

import jax
import jax.numpy as jnp
from jax import lax
from jax.experimental import pallas as pl
from jax.experimental.pallas import tpu as pltpu
from jax.sharding import PartitionSpec as P

LOG2E = math.log2(math.e)
MIB = 1 << 20
F32 = jnp.float32
BF16 = jnp.bfloat16
EXTRA = 16


def lane_group_mask(per_row, width):
    sub = lax.broadcasted_iota(jnp.int32, (per_row, width), 0)
    lane = lax.broadcasted_iota(jnp.int32, (per_row, width), 1)
    return (lane % per_row) == sub


def pack_kernel(cap, per_row, code_ref, q_ref, out_ref, place_ref, count_ref):
    owners = count_ref.shape[0] // 2
    rows = place_ref.shape[0]
    block = cap * per_row + EXTRA
    line = code_ref.shape[1]
    for i in range(2 * owners):
        count_ref[i] = 0

    def clear(i, carry):
        out_ref[pl.ds(pl.multiple_of(i * block, EXTRA), block), :] = jnp.zeros((block, 128), BF16)
        return carry

    lax.fori_loop(0, owners, clear, 0)

    def one(r, carry):
        group = lax.shift_right_logical(code_ref[r // line, r % line], 8)
        taken = count_ref[group]
        count_ref[group] = taken + 1
        owner = lax.shift_right_logical(group, 1)
        slot = jnp.where((group & 1) == 1, cap - 1 - taken, taken)
        place_ref[r] = owner * cap + slot
        start = pl.multiple_of(owner * block + slot * per_row, 16)
        out_ref[pl.ds(start, per_row), :] = q_ref[pl.ds(pl.multiple_of(r * per_row, per_row), per_row), :]
        return carry

    lax.fori_loop(0, rows, one, 0, unroll=8)
    lane = lax.broadcasted_iota(jnp.int32, (EXTRA, 128), 1)
    for o in range(owners):
        first = count_ref[2 * o].astype(F32)
        second = count_ref[2 * o + 1].astype(F32)
        out_ref[o * block + cap * per_row:(o + 1) * block, :] = jnp.where(lane < 64, first, second).astype(BF16)


def tail_kernel(steps, per_row, batch, scale, code_ref, q_ref, tk_ref, tv_ref, nk_ref, nv_ref, out_ref, lse_ref):
    base = pl.program_id(0) * batch
    line = code_ref.shape[1]
    slots = tk_ref.shape[0] // batch
    heads = per_row // steps
    total_rows = batch * per_row
    q = q_ref[...]
    parts = []
    lane = lax.broadcasted_iota(jnp.int32, (per_row, slots), 1)
    for i in range(batch):
        r = base + i
        length = code_ref[r // line, r % line] & 255
        s = lax.dot_general(
            q[i * per_row:(i + 1) * per_row], tk_ref[i * slots:(i + 1) * slots, :],
            (((1,), (1,)), ((), ())), preferred_element_type=F32,
        )
        parts.append(jnp.where(lane < length, s, -jnp.inf))
    st = jnp.concatenate(parts, axis=0)
    sn = lax.dot_general(q, nk_ref[...], (((1,), (1,)), ((), ())), preferred_element_type=F32)
    row = lax.broadcasted_iota(jnp.int32, sn.shape, 0)
    col = lax.broadcasted_iota(jnp.int32, sn.shape, 1)
    own = (row // per_row) == (col // steps)
    causal = (col % steps) <= ((row % per_row) // heads)
    sn = jnp.where(own & causal, sn, -jnp.inf)
    top = jnp.maximum(jnp.max(st, axis=1, keepdims=True), jnp.max(sn, axis=1, keepdims=True))
    et = jnp.exp2((st - top) * (scale * LOG2E))
    en = jnp.exp2((sn - top) * (scale * LOG2E))
    total = jnp.sum(et, axis=1, keepdims=True) + jnp.sum(en, axis=1, keepdims=True)
    pt = et.astype(BF16)
    summed = jnp.concatenate(
        [
            jnp.dot(pt[i * per_row:(i + 1) * per_row], tv_ref[i * slots:(i + 1) * slots, :], preferred_element_type=F32)
            for i in range(batch)
        ],
        axis=0,
    )
    summed = summed + jnp.dot(en.astype(BF16), nv_ref[...], preferred_element_type=F32)
    out_ref[...] = summed / total
    lse = top * scale + jnp.log(total)
    mask = lane_group_mask(per_row, 128)
    for i in range(batch):
        one = jnp.where(mask, lse[i * per_row:(i + 1) * per_row], 0.0)
        lse_ref[i:i + 1, :] = jnp.sum(one, axis=0, keepdims=True)


def prefix_kernel(cap, per_row, pref, scale, x_ref, k_ref, v_ref, out_ref, wide_ref, meta_ref, lse_ref, count_ref, list_ref, sem):
    block = cap * per_row + EXTRA
    sources = x_ref.shape[0] // block
    data = cap * per_row
    lane = lax.broadcasted_iota(jnp.int32, (1, 128), 1)
    for s in range(sources):
        tile = x_ref[s * block + data:(s + 1) * block, :].astype(F32)
        meta_ref[s:s + 1, :] = tile[0:1, :].astype(jnp.int32)
    copy = pltpu.make_async_copy(meta_ref, count_ref, sem)
    copy.start()
    groups = v_ref.shape[0] // pref
    wide_ref[:, 0:128] = v_ref[...]
    wide_ref[:, 128:256] = jnp.ones((groups * pref, 128), BF16)
    lse_ref[...] = jnp.zeros(lse_ref.shape, F32)
    copy.wait()
    found = []
    for g in range(2):
        at = jnp.int32(0)
        for s in range(sources):
            for i in range(cap):
                list_ref[g, at + i] = s * cap + (i if g == 0 else cap - 1 - i)
            at = at + count_ref[s, 64 * g]
        found.append(at)
        last = list_ref[g, jnp.maximum(at - 1, 0)]
        for i in range(cap):
            list_ref[g, at + i] = last
    first_blocks = (found[0] + 7) // 8
    blocks = first_blocks + (found[1] + 7) // 8
    mask = lane_group_mask(per_row, 128)

    def one(b, carry):
        g = (b >= first_blocks).astype(jnp.int32)
        j = (b - g * first_blocks) * 8
        slots = [list_ref[g, j + i] for i in range(8)]
        starts = [pl.multiple_of((s // cap) * block + (s % cap) * per_row, 16) for s in slots]
        q = jnp.concatenate([x_ref[pl.ds(a, per_row), :] for a in starts], axis=0)
        here = pl.multiple_of(g * pref, pref)
        score = lax.dot_general(
            q, k_ref[pl.ds(here, pref), :], (((1,), (1,)), ((), ())), preferred_element_type=F32
        )
        top = jnp.max(score, axis=1, keepdims=True)
        expo = jnp.exp2((score - top) * (scale * LOG2E)).astype(BF16)
        both = jnp.dot(expo, wide_ref[pl.ds(here, pref), :], preferred_element_type=F32)
        total = both[:, 128:256]
        result = (both[:, 0:128] / total).astype(BF16)
        lse = top * scale + jnp.log(total)
        for i in range(8):
            part = slice(i * per_row, (i + 1) * per_row)
            out_ref[pl.ds(starts[i], per_row), :] = result[part]
            lse_ref[pl.ds(slots[i], 1), :] = jnp.sum(jnp.where(mask, lse[part], 0.0), axis=0, keepdims=True)
        return carry

    lax.fori_loop(0, blocks, one, 0)
    for s in range(sources):
        full = lse_ref[s * cap:(s + 1) * cap, :]
        high = full.astype(BF16).astype(F32)
        rest = full - high
        mid = rest.astype(BF16).astype(F32)
        low = rest - mid
        lanes = lax.broadcasted_iota(jnp.int32, full.shape, 1)
        sent = jnp.where(lanes < per_row, high, jnp.where(lanes < 2 * per_row, mid, low))
        sent = jnp.concatenate([sent, jnp.zeros((EXTRA - cap, 128), F32)], axis=0)
        out_ref[s * block + data:(s + 1) * block, :] = sent.astype(BF16)


def merge_kernel(cap, per_row, batch, place_ref, x_ref, tail_ref, lse_ref, out_ref, sent_ref):
    block = cap * per_row + EXTRA
    owners = x_ref.shape[0] // block
    step = pl.program_id(0)

    @pl.when(step == 0)
    def _():
        for o in range(owners):
            tile = x_ref[o * block + cap * per_row:(o + 1) * block, :].astype(F32)
            sent_ref[o * cap:(o + 1) * cap, :] = tile[0:cap, :]

    mask = lane_group_mask(per_row, 128)
    lane = lax.broadcasted_iota(jnp.int32, (1, 128), 1)

    def one(i, carry):
        place = place_ref[step * batch + i]
        start = pl.multiple_of((place // cap) * block + (place % cap) * per_row, 16)
        terms = jnp.where(lane < 3 * per_row, sent_ref[pl.ds(place, 1), :], -lse_ref[pl.ds(i, 1), :])
        ahead = jnp.sum(jnp.where(mask, terms, 0.0), axis=1, keepdims=True)
        prefix = x_ref[pl.ds(start, per_row), :].astype(F32)
        here = pl.ds(pl.multiple_of(i * per_row, per_row), per_row)
        weight_p = 1.0 / (1.0 + jnp.exp(-ahead))
        weight_t = 1.0 / (1.0 + jnp.exp(ahead))
        out_ref[here, :] = (weight_p * prefix + weight_t * tail_ref[here, :]).astype(BF16)
        return carry

    lax.fori_loop(0, batch, one, 0, unroll=8)


def vmem():
    return pl.BlockSpec(memory_space=pltpu.VMEM)


def smem():
    return pl.BlockSpec(memory_space=pltpu.SMEM)


def body(
    queries, new_keys, new_values, tail_keys, tail_values, prefix_keys, prefix_values, route_owner, group_slot, tail_len
):
    rows, steps, heads, width = queries.shape
    owners = lax.axis_size("roll")
    cap = 8
    per_row = steps * heads
    scale = 1.0 / math.sqrt(width)
    slots = tail_keys.shape[2]
    pref = prefix_keys.shape[2]
    groups = prefix_keys.shape[0]
    block = cap * per_row + EXTRA
    code = (route_owner * 2 + group_slot) * 256 + tail_len
    codes = lax.all_gather(code, "tp", axis=0, tiled=True)
    flat = queries.reshape(rows * per_row, width)
    params = functools.partial(pltpu.CompilerParams, vmem_limit_bytes=32 * MIB)

    sent, place = pl.pallas_call(
        functools.partial(pack_kernel, cap, per_row),
        out_shape=(
            jax.ShapeDtypeStruct((owners * block, width), BF16),
            jax.ShapeDtypeStruct((rows,), jnp.int32),
        ),
        in_specs=[smem(), vmem()],
        out_specs=(vmem(), smem()),
        scratch_shapes=[pltpu.SMEM((2 * owners,), jnp.int32)],
        compiler_params=params(),
        cost_estimate=pl.CostEstimate(flops=0, bytes_accessed=3 * MIB, transcendentals=0),
        name="pack",
    )(codes, flat)
    arrived = lax.all_to_all(sent.reshape(owners, block, width), "roll", split_axis=0, concat_axis=0, tiled=True)

    batch = 8
    part = batch * per_row
    tail_out, tail_lse = pl.pallas_call(
        functools.partial(tail_kernel, steps, per_row, batch, scale),
        out_shape=(
            jax.ShapeDtypeStruct((rows * per_row, width), F32),
            jax.ShapeDtypeStruct((rows, 128), F32),
        ),
        grid=(rows // batch,),
        in_specs=[
            smem(),
            pl.BlockSpec((part, width), lambda i: (i, 0)),
            pl.BlockSpec((batch * slots, width), lambda i: (i, 0)),
            pl.BlockSpec((batch * slots, width), lambda i: (i, 0)),
            pl.BlockSpec((batch * steps, width), lambda i: (i, 0)),
            pl.BlockSpec((batch * steps, width), lambda i: (i, 0)),
        ],
        out_specs=(
            pl.BlockSpec((part, width), lambda i: (i, 0)),
            pl.BlockSpec((batch, 128), lambda i: (i, 0)),
        ),
        compiler_params=params(),
        cost_estimate=pl.CostEstimate(
            flops=4 * rows * per_row * slots * width, bytes_accessed=12 * MIB, transcendentals=rows * per_row * slots
        ),
        name="tail",
    )(
        codes, flat, tail_keys.reshape(rows * slots, width), tail_values.reshape(rows * slots, width),
        new_keys.reshape(rows * steps, width), new_values.reshape(rows * steps, width),
    )

    answered = pl.pallas_call(
        functools.partial(prefix_kernel, cap, per_row, pref, scale),
        out_shape=jax.ShapeDtypeStruct((owners * block, width), BF16),
        in_specs=[vmem(), vmem(), vmem()],
        out_specs=vmem(),
        scratch_shapes=[
            pltpu.VMEM((groups * pref, 2 * width), BF16),
            pltpu.VMEM((owners, 128), jnp.int32),
            pltpu.VMEM((owners * cap, 128), F32),
            pltpu.SMEM((owners, 128), jnp.int32),
            pltpu.SMEM((2, owners * cap + 2 * cap), jnp.int32),
            pltpu.SemaphoreType.DMA,
        ],
        compiler_params=params(),
        cost_estimate=pl.CostEstimate(
            flops=4 * owners * cap * per_row * pref * width, bytes_accessed=6 * MIB,
            transcendentals=owners * cap * per_row * pref,
        ),
        name="prefix",
    )(
        arrived.reshape(owners * block, width), prefix_keys.reshape(groups * pref, width),
        prefix_values.reshape(groups * pref, width),
    )
    back = lax.all_to_all(answered.reshape(owners, block, width), "roll", split_axis=0, concat_axis=0, tiled=True)

    batch = 32
    part = batch * per_row
    merged = pl.pallas_call(
        functools.partial(merge_kernel, cap, per_row, batch),
        out_shape=jax.ShapeDtypeStruct((rows * per_row, width), BF16),
        grid=(rows // batch,),
        in_specs=[
            smem(),
            pl.BlockSpec((owners * block, width), lambda i: (0, 0)),
            pl.BlockSpec((part, width), lambda i: (i, 0)),
            pl.BlockSpec((batch, 128), lambda i: (i, 0)),
        ],
        out_specs=pl.BlockSpec((part, width), lambda i: (i, 0)),
        scratch_shapes=[pltpu.VMEM((owners * cap, 128), F32)],
        compiler_params=params(),
        cost_estimate=pl.CostEstimate(flops=0, bytes_accessed=6 * MIB, transcendentals=0),
        name="merge",
    )(place, back.reshape(owners * block, width), tail_out, tail_lse)
    return merged.reshape(rows, steps, heads, width)


def solution(mesh):
    return jax.shard_map(
        body,
        mesh=mesh,
        in_specs=(
            P("roll", None, "tp", None),
            P("roll", None, "tp", None),
            P("roll", None, "tp", None),
            P("roll", "tp", None, None),
            P("roll", "tp", None, None),
            P("roll", "tp", None, None),
            P("roll", "tp", None, None),
            P("roll", "tp"),
            P("roll", "tp"),
            P("roll", "tp"),
        ),
        out_specs=P("roll", None, "tp", None),
        check_vma=False,
    )
```

```python
import functools
import math

import jax
import jax.numpy as jnp
from jax import lax
from jax.experimental import pallas as pl
from jax.experimental.pallas import tpu as pltpu
from jax.sharding import PartitionSpec as P

LOG2E = math.log2(math.e)
MIB = 1 << 20
F32 = jnp.float32
BF16 = jnp.bfloat16
EXTRA = 16


def lane_group_mask(per_row, width):
    sub = lax.broadcasted_iota(jnp.int32, (per_row, width), 0)
    lane = lax.broadcasted_iota(jnp.int32, (per_row, width), 1)
    return (lane % per_row) == sub


def pack_kernel(cap, per_row, code_ref, q_ref, out_ref, place_ref, held_ref, extra_ref, where_ref, sems):
    lines, line = code_ref.shape
    rows = lines * line
    owners = out_ref.shape[0]
    load = pltpu.make_async_copy(q_ref, held_ref, sems.at[0])
    load.start()
    group = lax.shift_right_logical(code_ref[...], 8).astype(F32).astype(BF16)
    z = lax.broadcasted_iota(jnp.int32, (lines, rows), 0)
    r = lax.broadcasted_iota(jnp.int32, (lines, rows), 1)
    j = lax.broadcasted_iota(jnp.int32, (line, rows), 0)
    rj = lax.broadcasted_iota(jnp.int32, (line, rows), 1)
    spread = jnp.dot(group, (rj % line == j).astype(BF16), preferred_element_type=F32)
    across = jnp.sum(jnp.where(r // line == z, spread, 0.0), axis=0, keepdims=True)
    rz = lax.broadcasted_iota(jnp.int32, (rows, lines), 0)
    zz = lax.broadcasted_iota(jnp.int32, (rows, lines), 1)
    picked = jnp.dot((rz // line == zz).astype(BF16), group, preferred_element_type=F32)
    rl = lax.broadcasted_iota(jnp.int32, (rows, line), 0)
    jl = lax.broadcasted_iota(jnp.int32, (rows, line), 1)
    picked = jnp.where(rl % line == jl, picked, 0.0).astype(BF16)
    down = jnp.dot(picked, jnp.ones((line, rows), BF16), preferred_element_type=F32)
    earlier = lax.broadcasted_iota(jnp.int32, (rows, rows), 0) < lax.broadcasted_iota(jnp.int32, (rows, rows), 1)
    rank = jnp.sum(jnp.where((down == across) & earlier, 1.0, 0.0), axis=0, keepdims=True).astype(jnp.int32)
    whole = across.astype(jnp.int32)
    slot = jnp.where((whole & 1) == 1, cap - 1 - rank, rank)
    place = lax.shift_right_logical(whole, 1) * cap + slot
    place_ref[...] = place
    index = pltpu.make_async_copy(place_ref, where_ref, sems.at[1])
    index.start()
    named = lax.broadcasted_iota(jnp.int32, (2 * owners, rows), 0).astype(F32) == across
    counts = jnp.dot(named.astype(BF16), jnp.ones((rows, 128), BF16), preferred_element_type=F32)
    half = EXTRA // 2
    for o in range(owners):
        first = jnp.broadcast_to(counts[2 * o:2 * o + 1, :], (half, 128))
        second = jnp.broadcast_to(counts[2 * o + 1:2 * o + 2, :], (half, 128))
        extra_ref[o] = jnp.concatenate([first, second], axis=0).astype(BF16)
    more = pltpu.make_async_copy(extra_ref, out_ref.at[:, pl.ds(cap * per_row, EXTRA), :], sems.at[2])
    more.start()
    index.wait()
    load.wait()

    def one(i, carry):
        at = where_ref[0, i]
        pltpu.make_async_copy(
            held_ref.at[pl.ds(pl.multiple_of(i * per_row, per_row), per_row), :],
            out_ref.at[lax.shift_right_logical(at, 3), pl.ds(pl.multiple_of((at & 7) * per_row, per_row), per_row), :],
            sems.at[0],
        ).start()
        return carry

    lax.fori_loop(0, rows, one, 0, unroll=8)
    more.wait()
    load.wait()


def tail_kernel(steps, per_row, batch, scale, code_ref, q_ref, tk_ref, tv_ref, nk_ref, nv_ref, out_ref, lse_ref):
    base = pl.program_id(0) * batch
    line = code_ref.shape[1]
    slots = tk_ref.shape[0] // batch
    heads = per_row // steps
    total_rows = batch * per_row
    q = q_ref[...]
    parts = []
    lane = lax.broadcasted_iota(jnp.int32, (per_row, slots), 1)
    for i in range(batch):
        r = base + i
        length = code_ref[r // line, r % line] & 255
        s = lax.dot_general(
            q[i * per_row:(i + 1) * per_row], tk_ref[i * slots:(i + 1) * slots, :],
            (((1,), (1,)), ((), ())), preferred_element_type=F32,
        )
        parts.append(jnp.where(lane < length, s, -jnp.inf))
    st = jnp.concatenate(parts, axis=0)
    sn = lax.dot_general(q, nk_ref[...], (((1,), (1,)), ((), ())), preferred_element_type=F32)
    row = lax.broadcasted_iota(jnp.int32, sn.shape, 0)
    col = lax.broadcasted_iota(jnp.int32, sn.shape, 1)
    own = (row // per_row) == (col // steps)
    causal = (col % steps) <= ((row % per_row) // heads)
    sn = jnp.where(own & causal, sn, -jnp.inf)
    top = jnp.maximum(jnp.max(st, axis=1, keepdims=True), jnp.max(sn, axis=1, keepdims=True))
    et = jnp.exp2((st - top) * (scale * LOG2E))
    en = jnp.exp2((sn - top) * (scale * LOG2E))
    total = jnp.sum(et, axis=1, keepdims=True) + jnp.sum(en, axis=1, keepdims=True)
    pt = et.astype(BF16)
    summed = jnp.concatenate(
        [
            jnp.dot(pt[i * per_row:(i + 1) * per_row], tv_ref[i * slots:(i + 1) * slots, :], preferred_element_type=F32)
            for i in range(batch)
        ],
        axis=0,
    )
    summed = summed + jnp.dot(en.astype(BF16), nv_ref[...], preferred_element_type=F32)
    out_ref[...] = summed / total
    lse = top * scale + jnp.log(total)
    mask = lane_group_mask(per_row, 128)
    for i in range(batch):
        one = jnp.where(mask, lse[i * per_row:(i + 1) * per_row], 0.0)
        lse_ref[i:i + 1, :] = jnp.sum(one, axis=0, keepdims=True)


def prefix_kernel(
    cap, per_row, pref, scale, x_ref, k_ref, v_ref, out_ref, held_ref, wide_ref, list_ref, lse_ref, sent_ref, where_ref, sems
):
    sources = x_ref.shape[0]
    data = cap * per_row
    groups = v_ref.shape[0] // pref
    half = EXTRA // 2
    i = lax.broadcasted_iota(jnp.int32, (sources, sources), 0)
    j = lax.broadcasted_iota(jnp.int32, (sources, sources), 1)
    lower = (j <= i).astype(BF16)
    lane = lax.broadcasted_iota(jnp.int32, (1, 128), 1)
    entries = []
    totals = []
    for g in range(2):
        count = jnp.concatenate(
            [x_ref[s, data:data + EXTRA, :].astype(F32)[g * half:g * half + 1, :] for s in range(sources)], axis=0
        )
        ends = jnp.dot(lower, count.astype(BF16), preferred_element_type=F32)
        total = ends[sources - 1:sources, :]
        totals.append(total)
        for h in range(2):
            at = jnp.maximum(jnp.minimum((lane + 128 * h).astype(F32), total - 1.0), 0.0)
            passed = ends <= at
            source = jnp.sum(jnp.where(passed, 1.0, 0.0), axis=0, keepdims=True)
            within = at - jnp.sum(jnp.where(passed, count, 0.0), axis=0, keepdims=True)
            entries.append(source * cap + (within if g == 0 else (cap - 1) - within))
    list_ref[...] = jnp.concatenate(entries + totals + totals, axis=0).astype(jnp.int32)
    copy = pltpu.make_async_copy(list_ref, where_ref, sems.at[0])
    copy.start()
    wide_ref[:, 0:128] = v_ref[...]
    wide_ref[:, 128:256] = jnp.ones((groups * pref, 128), BF16)
    lse_ref[...] = jnp.zeros(lse_ref.shape, F32)
    copy.wait()
    found = [where_ref[4, 0], where_ref[5, 0]]
    mask = lane_group_mask(per_row, 128)
    factor = scale * LOG2E

    def attend(unit, sub, shifted):
        first_units = (found[0] + unit - 1) // unit
        units = first_units + (found[1] + unit - 1) // unit

        def one(b, carry):
            g = (b >= first_units).astype(jnp.int32)
            j = (b - g * first_units) * unit
            row = 2 * g + lax.shift_right_logical(j, 7)
            first = j & 127
            slots = [where_ref[row, first + i] for i in range(unit)]
            own = [lax.shift_right_logical(s, 3) for s in slots]
            start = [pl.multiple_of((s & 7) * per_row, per_row) for s in slots]
            here = pl.multiple_of(g * pref, pref)
            scores = []
            for t in range(0, unit, sub):
                q = jnp.concatenate([x_ref[own[i], pl.ds(start[i], per_row), :] for i in range(t, t + sub)], axis=0)
                scores.append(
                    lax.dot_general(
                        q, k_ref[pl.ds(here, pref), :], (((1,), (1,)), ((), ())), preferred_element_type=F32
                    )
                )
            low, high = carry
            for t in range(0, unit, sub):
                score = scores[t // sub]
                top = jnp.max(score, axis=1, keepdims=True) if shifted else None
                expo = jnp.exp2((score - top if shifted else score) * factor).astype(BF16)
                both = jnp.dot(expo, wide_ref[pl.ds(here, pref), :], preferred_element_type=F32)
                total = both[:, 128:256]
                result = (both[:, 0:128] / total).astype(BF16)
                lse = jnp.log(total)
                if shifted:
                    lse = lse + top * scale
                stacked = total.reshape(sub * per_row // 8, 8, 128)
                low = jnp.minimum(low, jnp.min(stacked, axis=0))
                high = jnp.maximum(high, jnp.max(stacked, axis=0))
                for i in range(sub):
                    part = slice(i * per_row, (i + 1) * per_row)
                    held_ref[own[t + i], pl.ds(start[t + i], per_row), :] = result[part]
                    lse_ref[pl.ds(slots[t + i], 1), :] = jnp.sum(
                        jnp.where(mask, lse[part], 0.0), axis=0, keepdims=True
                    )
            return low, high

        return lax.fori_loop(0, units, one, (jnp.ones((8, 128), F32), jnp.ones((8, 128), F32)))

    low, high = attend(32, 8, False)
    safe = (jnp.min(low) > 2.0**-70) & (jnp.max(high) < 2.0**100)

    @pl.when(jnp.logical_not(safe))
    def _():
        attend(8, 8, True)

    for s in range(sources):
        full = lse_ref[s * cap:(s + 1) * cap, :]
        high_part = full.astype(BF16).astype(F32)
        rest = full - high_part
        mid_part = rest.astype(BF16).astype(F32)
        low_part = rest - mid_part
        lanes = lax.broadcasted_iota(jnp.int32, full.shape, 1)
        sent = jnp.where(lanes < per_row, high_part, jnp.where(lanes < 2 * per_row, mid_part, low_part))
        held_ref[s, data:data + EXTRA, :] = jnp.concatenate([sent, jnp.zeros_like(sent)], axis=0).astype(BF16)
    out = pltpu.make_async_copy(held_ref, out_ref, sems.at[0])
    out.start()
    out.wait()


def merge_kernel(cap, per_row, batch, place_ref, x_ref, tail_ref, lse_ref, out_ref, sent_ref, weight_ref):
    owners = x_ref.shape[0]
    data = cap * per_row
    step = pl.program_id(0)

    @pl.when(step == 0)
    def _():
        for o in range(owners):
            sent_ref[o * cap:(o + 1) * cap, :] = x_ref[o, data:data + EXTRA, :].astype(F32)[0:cap, :]

    mask = lane_group_mask(per_row, 128)
    lane = lax.broadcasted_iota(jnp.int32, (batch, 128), 1)
    places = [place_ref[0, step * batch + i] for i in range(batch)]
    lse = jnp.concatenate([sent_ref[pl.ds(p, 1), :] for p in places], axis=0)
    terms = jnp.where(lane < 3 * per_row, lse, -lse_ref[...])
    ahead = terms
    for k in range(1, 4):
        ahead = ahead + pltpu.roll(terms, k * per_row, 1)
    weight = 1.0 / (1.0 + jnp.exp(-ahead))
    high = weight.astype(BF16).astype(F32)
    mid = (weight - high).astype(BF16).astype(F32)
    weight_ref[...] = jnp.where(lane < per_row, high, jnp.where(lane < 2 * per_row, mid, jnp.where(lane < 3 * per_row, weight - high - mid, 0.0)))
    ones = jnp.ones((128, 128), BF16)
    for i in range(batch):
        place = places[i]
        spread = jnp.where(mask, weight_ref[i:i + 1, :], 0.0).astype(BF16)
        weight_p = jnp.dot(spread, ones, preferred_element_type=F32)
        start = pl.multiple_of((place & 7) * per_row, per_row)
        prefix = x_ref[lax.shift_right_logical(place, 3), pl.ds(start, per_row), :].astype(F32)
        tail = tail_ref[i * per_row:(i + 1) * per_row, :]
        out_ref[i * per_row:(i + 1) * per_row, :] = (tail + weight_p * (prefix - tail)).astype(BF16)


def vmem():
    return pl.BlockSpec(memory_space=pltpu.VMEM)


def hbm():
    return pl.BlockSpec(memory_space=pltpu.MemorySpace.HBM)


def smem():
    return pl.BlockSpec(memory_space=pltpu.SMEM)


def body(
    queries, new_keys, new_values, tail_keys, tail_values, prefix_keys, prefix_values, route_owner, group_slot, tail_len
):
    rows, steps, heads, width = queries.shape
    owners = lax.axis_size("roll")
    cap = 8
    per_row = steps * heads
    scale = 1.0 / math.sqrt(width)
    slots = tail_keys.shape[2]
    pref = prefix_keys.shape[2]
    groups = prefix_keys.shape[0]
    block = cap * per_row + EXTRA
    code = (route_owner * 2 + group_slot) * 256 + tail_len
    codes = lax.all_gather(code, "tp", axis=0, tiled=True)
    flat = queries.reshape(rows * per_row, width)
    params = functools.partial(pltpu.CompilerParams, vmem_limit_bytes=32 * MIB)

    sent, place = pl.pallas_call(
        functools.partial(pack_kernel, cap, per_row),
        out_shape=(
            jax.ShapeDtypeStruct((owners, block, width), BF16),
            jax.ShapeDtypeStruct((1, rows), jnp.int32),
        ),
        in_specs=[vmem(), hbm()],
        out_specs=(hbm(), vmem()),
        scratch_shapes=[
            pltpu.VMEM((rows * per_row, width), BF16),
            pltpu.VMEM((owners, EXTRA, 128), BF16),
            pltpu.SMEM((1, rows), jnp.int32),
            pltpu.SemaphoreType.DMA((3,)),
        ],
        compiler_params=params(),
        cost_estimate=pl.CostEstimate(flops=0, bytes_accessed=3 * MIB, transcendentals=0),
        name="pack",
    )(codes, flat)
    arrived = lax.all_to_all(sent, "roll", split_axis=0, concat_axis=0, tiled=True)

    batch = 8
    part = batch * per_row
    tail_out, tail_lse = pl.pallas_call(
        functools.partial(tail_kernel, steps, per_row, batch, scale),
        out_shape=(
            jax.ShapeDtypeStruct((rows * per_row, width), F32),
            jax.ShapeDtypeStruct((rows, 128), F32),
        ),
        grid=(rows // batch,),
        in_specs=[
            smem(),
            pl.BlockSpec((part, width), lambda i: (i, 0)),
            pl.BlockSpec((batch * slots, width), lambda i: (i, 0)),
            pl.BlockSpec((batch * slots, width), lambda i: (i, 0)),
            pl.BlockSpec((batch * steps, width), lambda i: (i, 0)),
            pl.BlockSpec((batch * steps, width), lambda i: (i, 0)),
        ],
        out_specs=(
            pl.BlockSpec((part, width), lambda i: (i, 0)),
            pl.BlockSpec((batch, 128), lambda i: (i, 0)),
        ),
        compiler_params=params(),
        cost_estimate=pl.CostEstimate(
            flops=4 * rows * per_row * slots * width, bytes_accessed=12 * MIB, transcendentals=rows * per_row * slots
        ),
        name="tail",
    )(
        codes, flat, tail_keys.reshape(rows * slots, width), tail_values.reshape(rows * slots, width),
        new_keys.reshape(rows * steps, width), new_values.reshape(rows * steps, width),
    )

    answered = pl.pallas_call(
        functools.partial(prefix_kernel, cap, per_row, pref, scale),
        out_shape=jax.ShapeDtypeStruct((owners, block, width), BF16),
        in_specs=[vmem(), vmem(), vmem()],
        out_specs=hbm(),
        scratch_shapes=[
            pltpu.VMEM((owners, block, width), BF16),
            pltpu.VMEM((groups * pref, 2 * width), BF16),
            pltpu.VMEM((8, 128), jnp.int32),
            pltpu.VMEM((owners * cap, 128), F32),
            pltpu.VMEM((owners * cap, 128), F32),
            pltpu.SMEM((8, 128), jnp.int32),
            pltpu.SemaphoreType.DMA((1,)),
        ],
        compiler_params=params(),
        cost_estimate=pl.CostEstimate(
            flops=4 * owners * cap * per_row * pref * width, bytes_accessed=6 * MIB,
            transcendentals=owners * cap * per_row * pref,
        ),
        name="prefix",
    )(arrived, prefix_keys.reshape(groups * pref, width), prefix_values.reshape(groups * pref, width))
    back = lax.all_to_all(answered, "roll", split_axis=0, concat_axis=0, tiled=True)

    batch = 32
    part = batch * per_row
    merged = pl.pallas_call(
        functools.partial(merge_kernel, cap, per_row, batch),
        out_shape=jax.ShapeDtypeStruct((rows * per_row, width), BF16),
        grid=(rows // batch,),
        in_specs=[
            smem(),
            pl.BlockSpec((owners, block, width), lambda i: (0, 0, 0)),
            pl.BlockSpec((part, width), lambda i: (i, 0)),
            pl.BlockSpec((batch, 128), lambda i: (i, 0)),
        ],
        out_specs=pl.BlockSpec((part, width), lambda i: (i, 0)),
        scratch_shapes=[pltpu.VMEM((owners * cap, 128), F32), pltpu.VMEM((batch, 128), F32)],
        compiler_params=params(),
        cost_estimate=pl.CostEstimate(flops=0, bytes_accessed=6 * MIB, transcendentals=0),
        name="merge",
    )(place, back, tail_out, tail_lse)
    return merged.reshape(rows, steps, heads, width)


def solution(mesh):
    return jax.shard_map(
        body,
        mesh=mesh,
        in_specs=(
            P("roll", None, "tp", None),
            P("roll", None, "tp", None),
            P("roll", None, "tp", None),
            P("roll", "tp", None, None),
            P("roll", "tp", None, None),
            P("roll", "tp", None, None),
            P("roll", "tp", None, None),
            P("roll", "tp"),
            P("roll", "tp"),
            P("roll", "tp"),
        ),
        out_specs=P("roll", None, "tp", None),
        check_vma=False,
    )
```

```python
import functools
import math

import jax
import jax.numpy as jnp
from jax import lax
from jax.experimental import pallas as pl
from jax.experimental.pallas import tpu as pltpu
from jax.sharding import PartitionSpec as P

LOG2E = math.log2(math.e)
MIB = 1 << 20
F32 = jnp.float32
BF16 = jnp.bfloat16
EXTRA = 16


def lane_group_mask(per_row, width):
    sub = lax.broadcasted_iota(jnp.int32, (per_row, width), 0)
    lane = lax.broadcasted_iota(jnp.int32, (per_row, width), 1)
    return (lane % per_row) == sub


def pack_kernel(cap, per_row, code_ref, q_ref, out_ref, place_ref, held_ref, extra_ref, where_ref, sems):
    lines, line = code_ref.shape
    rows = lines * line
    owners = out_ref.shape[0]
    load = pltpu.make_async_copy(q_ref, held_ref, sems.at[0])
    load.start()
    group = lax.shift_right_logical(code_ref[...], 8).astype(F32).astype(BF16)
    z = lax.broadcasted_iota(jnp.int32, (lines, rows), 0)
    r = lax.broadcasted_iota(jnp.int32, (lines, rows), 1)
    j = lax.broadcasted_iota(jnp.int32, (line, rows), 0)
    rj = lax.broadcasted_iota(jnp.int32, (line, rows), 1)
    spread = jnp.dot(group, (rj % line == j).astype(BF16), preferred_element_type=F32)
    across = jnp.sum(jnp.where(r // line == z, spread, 0.0), axis=0, keepdims=True)
    rz = lax.broadcasted_iota(jnp.int32, (rows, lines), 0)
    zz = lax.broadcasted_iota(jnp.int32, (rows, lines), 1)
    picked = jnp.dot((rz // line == zz).astype(BF16), group, preferred_element_type=F32)
    rl = lax.broadcasted_iota(jnp.int32, (rows, line), 0)
    jl = lax.broadcasted_iota(jnp.int32, (rows, line), 1)
    picked = jnp.where(rl % line == jl, picked, 0.0).astype(BF16)
    down = jnp.dot(picked, jnp.ones((line, rows), BF16), preferred_element_type=F32)
    earlier = lax.broadcasted_iota(jnp.int32, (rows, rows), 0) < lax.broadcasted_iota(jnp.int32, (rows, rows), 1)
    rank = jnp.sum(jnp.where((down == across) & earlier, 1.0, 0.0), axis=0, keepdims=True).astype(jnp.int32)
    whole = across.astype(jnp.int32)
    slot = jnp.where((whole & 1) == 1, cap - 1 - rank, rank)
    place = lax.shift_right_logical(whole, 1) * cap + slot
    place_ref[...] = place
    index = pltpu.make_async_copy(place_ref, where_ref, sems.at[1])
    index.start()
    named = lax.broadcasted_iota(jnp.int32, (2 * owners, rows), 0).astype(F32) == across
    counts = jnp.dot(named.astype(BF16), jnp.ones((rows, 128), BF16), preferred_element_type=F32)
    half = EXTRA // 2
    for o in range(owners):
        first = jnp.broadcast_to(counts[2 * o:2 * o + 1, :], (half, 128))
        second = jnp.broadcast_to(counts[2 * o + 1:2 * o + 2, :], (half, 128))
        extra_ref[o] = jnp.concatenate([first, second], axis=0).astype(BF16)
    more = pltpu.make_async_copy(extra_ref, out_ref.at[:, pl.ds(cap * per_row, EXTRA), :], sems.at[2])
    more.start()
    index.wait()
    load.wait()

    def one(i, carry):
        at = where_ref[0, i]
        pltpu.make_async_copy(
            held_ref.at[pl.ds(pl.multiple_of(i * per_row, per_row), per_row), :],
            out_ref.at[lax.shift_right_logical(at, 3), pl.ds(pl.multiple_of((at & 7) * per_row, per_row), per_row), :],
            sems.at[0],
        ).start()
        return carry

    lax.fori_loop(0, rows, one, 0, unroll=16)
    more.wait()
    load.wait()


def tail_kernel(steps, per_row, batch, scale, code_ref, q_ref, tk_ref, tv_ref, nk_ref, nv_ref, out_ref, lse_ref):
    base = pl.program_id(0) * batch
    line = code_ref.shape[1]
    slots = tk_ref.shape[0] // batch
    heads = per_row // steps
    total_rows = batch * per_row
    q = q_ref[...]
    parts = []
    lane = lax.broadcasted_iota(jnp.int32, (per_row, slots), 1)
    for i in range(batch):
        r = base + i
        length = code_ref[r // line, r % line] & 255
        s = lax.dot_general(
            q[i * per_row:(i + 1) * per_row], tk_ref[i * slots:(i + 1) * slots, :],
            (((1,), (1,)), ((), ())), preferred_element_type=F32,
        )
        parts.append(jnp.where(lane < length, s, -jnp.inf))
    st = jnp.concatenate(parts, axis=0)
    sn = lax.dot_general(q, nk_ref[...], (((1,), (1,)), ((), ())), preferred_element_type=F32)
    row = lax.broadcasted_iota(jnp.int32, sn.shape, 0)
    col = lax.broadcasted_iota(jnp.int32, sn.shape, 1)
    own = (row // per_row) == (col // steps)
    causal = (col % steps) <= ((row % per_row) // heads)
    sn = jnp.where(own & causal, sn, -jnp.inf)
    top = jnp.maximum(jnp.max(st, axis=1, keepdims=True), jnp.max(sn, axis=1, keepdims=True))
    et = jnp.exp2((st - top) * (scale * LOG2E))
    en = jnp.exp2((sn - top) * (scale * LOG2E))
    total = jnp.sum(et, axis=1, keepdims=True) + jnp.sum(en, axis=1, keepdims=True)
    pt = et.astype(BF16)
    summed = jnp.concatenate(
        [
            jnp.dot(pt[i * per_row:(i + 1) * per_row], tv_ref[i * slots:(i + 1) * slots, :], preferred_element_type=F32)
            for i in range(batch)
        ],
        axis=0,
    )
    summed = summed + jnp.dot(en.astype(BF16), nv_ref[...], preferred_element_type=F32)
    out_ref[...] = summed / total
    lse = top * scale + jnp.log(total)
    mask = lane_group_mask(per_row, 128)
    for i in range(batch):
        one = jnp.where(mask, lse[i * per_row:(i + 1) * per_row], 0.0)
        lse_ref[i:i + 1, :] = jnp.sum(one, axis=0, keepdims=True)


def prefix_kernel(
    cap, per_row, pref, scale, x_ref, k_ref, v_ref, out_ref, held_ref, wide_ref, list_ref, lse_ref, sent_ref, where_ref, sems
):
    sources = x_ref.shape[0]
    data = cap * per_row
    groups = v_ref.shape[0] // pref
    half = EXTRA // 2
    i = lax.broadcasted_iota(jnp.int32, (sources, sources), 0)
    j = lax.broadcasted_iota(jnp.int32, (sources, sources), 1)
    lower = (j <= i).astype(BF16)
    lane = lax.broadcasted_iota(jnp.int32, (1, 128), 1)
    entries = []
    totals = []
    for g in range(2):
        count = jnp.concatenate(
            [x_ref[s, data:data + EXTRA, :].astype(F32)[g * half:g * half + 1, :] for s in range(sources)], axis=0
        )
        ends = jnp.dot(lower, count.astype(BF16), preferred_element_type=F32)
        total = ends[sources - 1:sources, :]
        totals.append(total)
        for h in range(2):
            at = jnp.maximum(jnp.minimum((lane + 128 * h).astype(F32), total - 1.0), 0.0)
            passed = ends <= at
            source = jnp.sum(jnp.where(passed, 1.0, 0.0), axis=0, keepdims=True)
            within = at - jnp.sum(jnp.where(passed, count, 0.0), axis=0, keepdims=True)
            entries.append(source * cap + (within if g == 0 else (cap - 1) - within))
    list_ref[...] = jnp.concatenate(entries + totals + totals, axis=0).astype(jnp.int32)
    copy = pltpu.make_async_copy(list_ref, where_ref, sems.at[0])
    copy.start()
    wide_ref[:, 0:128] = v_ref[...]
    wide_ref[:, 128:256] = jnp.ones((groups * pref, 128), BF16)
    lse_ref[...] = jnp.zeros(lse_ref.shape, F32)
    copy.wait()
    found = [where_ref[4, 0], where_ref[5, 0]]
    mask = lane_group_mask(per_row, 128)
    factor = scale * LOG2E

    def attend(unit, sub, shifted):
        first_units = (found[0] + unit - 1) // unit
        units = first_units + (found[1] + unit - 1) // unit

        def one(b, carry):
            g = (b >= first_units).astype(jnp.int32)
            j = (b - g * first_units) * unit
            row = 2 * g + lax.shift_right_logical(j, 7)
            first = j & 127
            slots = [where_ref[row, first + i] for i in range(unit)]
            own = [lax.shift_right_logical(s, 3) for s in slots]
            start = [pl.multiple_of((s & 7) * per_row, per_row) for s in slots]
            here = pl.multiple_of(g * pref, pref)
            scores = []
            for t in range(0, unit, sub):
                q = jnp.concatenate([x_ref[own[i], pl.ds(start[i], per_row), :] for i in range(t, t + sub)], axis=0)
                scores.append(
                    lax.dot_general(
                        q, k_ref[pl.ds(here, pref), :], (((1,), (1,)), ((), ())), preferred_element_type=F32
                    )
                )
            low, high = carry
            for t in range(0, unit, sub):
                score = scores[t // sub]
                top = jnp.max(score, axis=1, keepdims=True) if shifted else None
                expo = jnp.exp2((score - top if shifted else score) * factor).astype(BF16)
                both = jnp.dot(expo, wide_ref[pl.ds(here, pref), :], preferred_element_type=F32)
                total = both[:, 128:256]
                result = (both[:, 0:128] / total).astype(BF16)
                lse = jnp.log(total)
                if shifted:
                    lse = lse + top * scale
                stacked = total.reshape(sub * per_row // 8, 8, 128)
                low = jnp.minimum(low, jnp.min(stacked, axis=0))
                high = jnp.maximum(high, jnp.max(stacked, axis=0))
                for i in range(sub):
                    part = slice(i * per_row, (i + 1) * per_row)
                    held_ref[own[t + i], pl.ds(start[t + i], per_row), :] = result[part]
                    lse_ref[pl.ds(slots[t + i], 1), :] = jnp.sum(
                        jnp.where(mask, lse[part], 0.0), axis=0, keepdims=True
                    )
            return low, high

        return lax.fori_loop(0, units, one, (jnp.ones((8, 128), F32), jnp.ones((8, 128), F32)))

    low, high = attend(32, 8, False)
    safe = (jnp.min(low) > 2.0**-70) & (jnp.max(high) < 2.0**100)

    @pl.when(jnp.logical_not(safe))
    def _():
        attend(8, 8, True)

    for s in range(sources):
        full = lse_ref[s * cap:(s + 1) * cap, :]
        high_part = full.astype(BF16).astype(F32)
        rest = full - high_part
        mid_part = rest.astype(BF16).astype(F32)
        low_part = rest - mid_part
        lanes = lax.broadcasted_iota(jnp.int32, full.shape, 1)
        sent = jnp.where(lanes < per_row, high_part, jnp.where(lanes < 2 * per_row, mid_part, low_part))
        held_ref[s, data:data + EXTRA, :] = jnp.concatenate([sent, jnp.zeros_like(sent)], axis=0).astype(BF16)
    out = pltpu.make_async_copy(held_ref, out_ref, sems.at[0])
    out.start()
    out.wait()


def merge_kernel(cap, per_row, chunks, place_ref, x_ref, lse_ref, tail_ref, out_ref, sent_ref, weight_ref, done_ref, sems):
    owners = x_ref.shape[0]
    data = cap * per_row
    rows = lse_ref.shape[0]
    batch = rows // chunks
    part = batch * per_row

    def piece(ref, c):
        return ref.at[pl.ds(c * part, part), :]

    stores = [pltpu.make_async_copy(piece(done_ref, c), piece(out_ref, c), sems.at[c]) for c in range(chunks)]
    for o in range(owners):
        sent_ref[o * cap:(o + 1) * cap, :] = x_ref[o, data:data + EXTRA, :].astype(F32)[0:cap, :]
    mask = lane_group_mask(per_row, 128)
    lane = lax.broadcasted_iota(jnp.int32, (batch, 128), 1)
    ones = jnp.ones((128, 128), BF16)
    for c in range(chunks):
        places = [place_ref[0, c * batch + i] for i in range(batch)]
        lse = jnp.concatenate([sent_ref[pl.ds(p, 1), :] for p in places], axis=0)
        terms = jnp.where(lane < 3 * per_row, lse, -lse_ref[c * batch:(c + 1) * batch, :])
        ahead = terms
        for k in range(1, 4):
            ahead = ahead + pltpu.roll(terms, k * per_row, 1)
        weight = 1.0 / (1.0 + jnp.exp(-ahead))
        high = weight.astype(BF16).astype(F32)
        rest = weight - high
        mid = rest.astype(BF16).astype(F32)
        low = jnp.where(lane < 3 * per_row, rest - mid, 0.0)
        weight_ref[c * batch:(c + 1) * batch, :] = jnp.where(lane < per_row, high, jnp.where(lane < 2 * per_row, mid, low))
        spread = jnp.concatenate(
            [jnp.where(mask, weight_ref[c * batch + i:c * batch + i + 1, :], 0.0).astype(BF16) for i in range(batch)], axis=0
        )
        weight_p = jnp.dot(spread, ones, preferred_element_type=F32)
        for i in range(batch):
            here = slice(i * per_row, (i + 1) * per_row)
            there = slice(c * part + i * per_row, c * part + (i + 1) * per_row)
            start = pl.multiple_of((places[i] & 7) * per_row, per_row)
            prefix = x_ref[lax.shift_right_logical(places[i], 3), pl.ds(start, per_row), :].astype(F32)
            tail = tail_ref[there, :]
            done_ref[there, :] = (tail + weight_p[here] * (prefix - tail)).astype(BF16)
        stores[c].start()
    for store in stores:
        store.wait()


def vmem():
    return pl.BlockSpec(memory_space=pltpu.VMEM)


def hbm():
    return pl.BlockSpec(memory_space=pltpu.MemorySpace.HBM)


def in_vmem(x):
    return pltpu.with_memory_space_constraint(x, pltpu.VMEM)


def in_hbm(x):
    return pltpu.with_memory_space_constraint(x, pltpu.HBM)


def smem():
    return pl.BlockSpec(memory_space=pltpu.SMEM)


def body(
    queries, new_keys, new_values, tail_keys, tail_values, prefix_keys, prefix_values, route_owner, group_slot, tail_len
):
    rows, steps, heads, width = queries.shape
    owners = lax.axis_size("roll")
    cap = 8
    per_row = steps * heads
    scale = 1.0 / math.sqrt(width)
    slots = tail_keys.shape[2]
    pref = prefix_keys.shape[2]
    groups = prefix_keys.shape[0]
    block = cap * per_row + EXTRA
    code = (route_owner * 2 + group_slot) * 256 + tail_len
    codes = lax.all_gather(code, "tp", axis=0, tiled=True)
    flat = queries.reshape(rows * per_row, width)
    params = functools.partial(pltpu.CompilerParams, vmem_limit_bytes=32 * MIB)

    sent, place = pl.pallas_call(
        functools.partial(pack_kernel, cap, per_row),
        out_shape=(
            pltpu.HBM((owners, block, width), BF16),
            jax.ShapeDtypeStruct((1, rows), jnp.int32),
        ),
        in_specs=[vmem(), hbm()],
        out_specs=(hbm(), vmem()),
        scratch_shapes=[
            pltpu.VMEM((rows * per_row, width), BF16),
            pltpu.VMEM((owners, EXTRA, 128), BF16),
            pltpu.SMEM((1, rows), jnp.int32),
            pltpu.SemaphoreType.DMA((3,)),
        ],
        compiler_params=params(),
        cost_estimate=pl.CostEstimate(flops=0, bytes_accessed=3 * MIB, transcendentals=0),
        name="pack",
    )(codes, in_hbm(flat))
    arrived = lax.all_to_all(sent, "roll", split_axis=0, concat_axis=0, tiled=True)

    batch = 8
    part = batch * per_row
    tail_out, tail_lse = pl.pallas_call(
        functools.partial(tail_kernel, steps, per_row, batch, scale),
        out_shape=(
            pltpu.VMEM((rows * per_row, width), F32),
            pltpu.VMEM((rows, 128), F32),
        ),
        grid=(rows // batch,),
        in_specs=[
            smem(),
            pl.BlockSpec((part, width), lambda i: (i, 0)),
            pl.BlockSpec((batch * slots, width), lambda i: (i, 0)),
            pl.BlockSpec((batch * slots, width), lambda i: (i, 0)),
            pl.BlockSpec((batch * steps, width), lambda i: (i, 0)),
            pl.BlockSpec((batch * steps, width), lambda i: (i, 0)),
        ],
        out_specs=(
            pl.BlockSpec((part, width), lambda i: (i, 0)),
            pl.BlockSpec((batch, 128), lambda i: (i, 0)),
        ),
        compiler_params=params(),
        cost_estimate=pl.CostEstimate(
            flops=4 * rows * per_row * slots * width, bytes_accessed=12 * MIB, transcendentals=rows * per_row * slots
        ),
        name="tail",
    )(
        codes, in_hbm(flat), in_hbm(tail_keys.reshape(rows * slots, width)), in_hbm(tail_values.reshape(rows * slots, width)),
        new_keys.reshape(rows * steps, width), new_values.reshape(rows * steps, width),
    )

    answered = pl.pallas_call(
        functools.partial(prefix_kernel, cap, per_row, pref, scale),
        out_shape=pltpu.HBM((owners, block, width), BF16),
        in_specs=[vmem(), vmem(), vmem()],
        out_specs=hbm(),
        scratch_shapes=[
            pltpu.VMEM((owners, block, width), BF16),
            pltpu.VMEM((groups * pref, 2 * width), BF16),
            pltpu.VMEM((8, 128), jnp.int32),
            pltpu.VMEM((owners * cap, 128), F32),
            pltpu.VMEM((owners * cap, 128), F32),
            pltpu.SMEM((8, 128), jnp.int32),
            pltpu.SemaphoreType.DMA((1,)),
        ],
        compiler_params=params(),
        cost_estimate=pl.CostEstimate(
            flops=4 * owners * cap * per_row * pref * width, bytes_accessed=6 * MIB,
            transcendentals=owners * cap * per_row * pref,
        ),
        name="prefix",
    )(arrived, prefix_keys.reshape(groups * pref, width), prefix_values.reshape(groups * pref, width))
    back = lax.all_to_all(answered, "roll", split_axis=0, concat_axis=0, tiled=True)

    chunks = 4
    merged = pl.pallas_call(
        functools.partial(merge_kernel, cap, per_row, chunks),
        out_shape=pltpu.HBM((rows * per_row, width), BF16),
        in_specs=[smem(), vmem(), vmem(), vmem()],
        out_specs=hbm(),
        scratch_shapes=[
            pltpu.VMEM((owners * cap, 128), F32),
            pltpu.VMEM((rows, 128), F32),
            pltpu.VMEM((rows * per_row, width), BF16),
            pltpu.SemaphoreType.DMA((chunks,)),
        ],
        compiler_params=params(),
        cost_estimate=pl.CostEstimate(flops=0, bytes_accessed=6 * MIB, transcendentals=0),
        name="merge",
    )(place, in_vmem(back), in_vmem(tail_lse), in_vmem(tail_out))
    return merged.reshape(rows, steps, heads, width)


def solution(mesh):
    return jax.shard_map(
        body,
        mesh=mesh,
        in_specs=(
            P("roll", None, "tp", None),
            P("roll", None, "tp", None),
            P("roll", None, "tp", None),
            P("roll", "tp", None, None),
            P("roll", "tp", None, None),
            P("roll", "tp", None, None),
            P("roll", "tp", None, None),
            P("roll", "tp"),
            P("roll", "tp"),
            P("roll", "tp"),
        ),
        out_specs=P("roll", None, "tp", None),
        check_vma=False,
    )
```

```python
import functools
import math

import jax
import jax.numpy as jnp
from jax import lax
from jax.experimental import pallas as pl
from jax.experimental.pallas import tpu as pltpu
from jax.sharding import PartitionSpec as P

LOG2E = math.log2(math.e)
MIB = 1 << 20
F32 = jnp.float32
BF16 = jnp.bfloat16
EXTRA = 16


def lane_group_mask(per_row, width):
    sub = lax.broadcasted_iota(jnp.int32, (per_row, width), 0)
    lane = lax.broadcasted_iota(jnp.int32, (per_row, width), 1)
    return (lane % per_row) == sub


def pack_kernel(cap, per_row, code_ref, q_ref, out_ref, place_ref, held_ref, extra_ref, where_ref, sems):
    lines, line = code_ref.shape
    rows = lines * line
    owners = out_ref.shape[0]
    load = pltpu.make_async_copy(q_ref, held_ref, sems.at[0])
    load.start()
    group = lax.shift_right_logical(code_ref[...], 8).astype(F32).astype(BF16)
    z = lax.broadcasted_iota(jnp.int32, (lines, rows), 0)
    r = lax.broadcasted_iota(jnp.int32, (lines, rows), 1)
    j = lax.broadcasted_iota(jnp.int32, (line, rows), 0)
    rj = lax.broadcasted_iota(jnp.int32, (line, rows), 1)
    spread = jnp.dot(group, (rj % line == j).astype(BF16), preferred_element_type=F32)
    across = jnp.sum(jnp.where(r // line == z, spread, 0.0), axis=0, keepdims=True)
    rz = lax.broadcasted_iota(jnp.int32, (rows, lines), 0)
    zz = lax.broadcasted_iota(jnp.int32, (rows, lines), 1)
    picked = jnp.dot((rz // line == zz).astype(BF16), group, preferred_element_type=F32)
    rl = lax.broadcasted_iota(jnp.int32, (rows, line), 0)
    jl = lax.broadcasted_iota(jnp.int32, (rows, line), 1)
    picked = jnp.where(rl % line == jl, picked, 0.0).astype(BF16)
    down = jnp.dot(picked, jnp.ones((line, rows), BF16), preferred_element_type=F32)
    across = across.astype(jnp.int32)
    down = down.astype(jnp.int32)
    sub = lax.broadcasted_iota(jnp.int32, (rows, rows), 0)
    lane = lax.broadcasted_iota(jnp.int32, (rows, rows), 1)
    chip = lax.shift_right_logical(across, 2)
    shared = lax.shift_right_logical(down, 2) == chip
    before = shared & (down * rows + sub < across * rows + lane)
    rank = jnp.sum(jnp.where(before, 1.0, 0.0), axis=0, keepdims=True).astype(jnp.int32)
    number = jnp.sum(jnp.where(shared, 1.0, 0.0), axis=0, keepdims=True).astype(jnp.int32)
    half = lax.shift_right_logical(number + 1, 1)
    core = (rank >= half).astype(jnp.int32)
    device = chip * 2 + core
    place = device * cap + rank - core * half
    place_ref[...] = place
    index = pltpu.make_async_copy(place_ref, where_ref, sems.at[1])
    index.start()
    named = lax.broadcasted_iota(jnp.int32, (4 * owners, rows), 0) == device * 4 + (across & 3)
    counts = jnp.dot(named.astype(BF16), jnp.ones((rows, 128), BF16), preferred_element_type=F32).astype(BF16)
    ii = lax.broadcasted_iota(jnp.int32, (owners * EXTRA, 4 * owners), 0)
    kk = lax.broadcasted_iota(jnp.int32, (owners * EXTRA, 4 * owners), 1)
    repeat = (lax.shift_right_logical(ii, 2) == kk).astype(BF16)
    extra_ref[...] = jnp.dot(repeat, counts, preferred_element_type=F32).astype(BF16).reshape(owners, EXTRA, 128)
    more = pltpu.make_async_copy(extra_ref, out_ref.at[:, pl.ds(cap * per_row, EXTRA), :], sems.at[2])
    more.start()
    index.wait()
    load.wait()

    def one(i, carry):
        at = where_ref[0, i]
        pltpu.make_async_copy(
            held_ref.at[pl.ds(pl.multiple_of(i * per_row, per_row), per_row), :],
            out_ref.at[lax.shift_right_logical(at, 3), pl.ds(pl.multiple_of((at & 7) * per_row, per_row), per_row), :],
            sems.at[0],
        ).start()
        return carry

    lax.fori_loop(0, rows, one, 0, unroll=16)
    more.wait()
    load.wait()


def tail_kernel(steps, per_row, batch, scale, code_ref, q_ref, tk_ref, tv_ref, nk_ref, nv_ref, out_ref, lse_ref):
    base = pl.program_id(0) * batch
    line = code_ref.shape[1]
    slots = tk_ref.shape[0] // batch
    heads = per_row // steps
    total_rows = batch * per_row
    q = q_ref[...]
    parts = []
    lane = lax.broadcasted_iota(jnp.int32, (per_row, slots), 1)
    for i in range(batch):
        r = base + i
        length = code_ref[r // line, r % line] & 255
        s = lax.dot_general(
            q[i * per_row:(i + 1) * per_row], tk_ref[i * slots:(i + 1) * slots, :],
            (((1,), (1,)), ((), ())), preferred_element_type=F32,
        )
        parts.append(jnp.where(lane < length, s, -jnp.inf))
    st = jnp.concatenate(parts, axis=0)
    sn = lax.dot_general(q, nk_ref[...], (((1,), (1,)), ((), ())), preferred_element_type=F32)
    row = lax.broadcasted_iota(jnp.int32, sn.shape, 0)
    col = lax.broadcasted_iota(jnp.int32, sn.shape, 1)
    own = (row // per_row) == (col // steps)
    causal = (col % steps) <= ((row % per_row) // heads)
    sn = jnp.where(own & causal, sn, -jnp.inf)
    top = jnp.maximum(jnp.max(st, axis=1, keepdims=True), jnp.max(sn, axis=1, keepdims=True))
    et = jnp.exp2((st - top) * (scale * LOG2E))
    en = jnp.exp2((sn - top) * (scale * LOG2E))
    total = jnp.sum(et, axis=1, keepdims=True) + jnp.sum(en, axis=1, keepdims=True)
    pt = et.astype(BF16)
    summed = jnp.concatenate(
        [
            jnp.dot(pt[i * per_row:(i + 1) * per_row], tv_ref[i * slots:(i + 1) * slots, :], preferred_element_type=F32)
            for i in range(batch)
        ],
        axis=0,
    )
    summed = summed + jnp.dot(en.astype(BF16), nv_ref[...], preferred_element_type=F32)
    out_ref[...] = summed / total
    lse = top * scale + jnp.log(total)
    mask = lane_group_mask(per_row, 128)
    for i in range(batch):
        one = jnp.where(mask, lse[i * per_row:(i + 1) * per_row], 0.0)
        lse_ref[i:i + 1, :] = jnp.sum(one, axis=0, keepdims=True)


def prefix_kernel(
    cap, per_row, pref, scale, x_ref, k_ref, v_ref, ko_ref, vo_ref, out_ref, key_ref, wide_ref, list_ref, lse_ref,
    where_ref, sems
):
    sources = x_ref.shape[0]
    data = cap * per_row
    own_rows = k_ref.shape[0]
    i = lax.broadcasted_iota(jnp.int32, (sources, sources), 0)
    j = lax.broadcasted_iota(jnp.int32, (sources, sources), 1)
    lower = (j <= i).astype(BF16)
    source = lax.broadcasted_iota(jnp.int32, (sources, 128), 0).astype(F32)
    lane = lax.broadcasted_iota(jnp.int32, (1, 128), 1).astype(F32)
    tiles = [x_ref[s, data:data + EXTRA, :].astype(F32) for s in range(sources)]
    fore = jnp.zeros((sources, 128), F32)
    end = jnp.zeros((1, 128), F32)
    tables = []
    for g in range(4):
        count = jnp.concatenate([tile[4 * g:4 * g + 1, :] for tile in tiles], axis=0)
        ends = jnp.dot(lower, count.astype(BF16), preferred_element_type=F32)
        total = ends[sources - 1:sources, :]
        tables.append((end, total, ends - count, ends, source * cap + fore))
        fore = fore + count
        end = end + jnp.floor((total + 7.0) * 0.125) * 8.0
    lists = []
    for h in range(3):
        p = jnp.minimum(lane + 128.0 * h, end - 1.0)
        entry = jnp.zeros((1, 128), F32)
        for g, (base, total, begins, ends, first) in enumerate(tables):
            at = jnp.maximum(jnp.minimum(p - base, total - 1.0), 0.0)
            mine = (begins <= at) & (at < ends)
            slot = jnp.sum(jnp.where(mine, first + at - begins, 0.0), axis=0, keepdims=True)
            entry = jnp.where((p >= base) & (total > 0.0), slot + 256.0 * g, entry)
        lists.append(entry)
    list_ref[...] = jnp.concatenate(lists + [end] + lists + [end], axis=0).astype(jnp.int32)
    copy = pltpu.make_async_copy(list_ref, where_ref, sems.at[0])
    copy.start()
    core = lax.axis_index("roll") & 1
    mine = pl.ds(pl.multiple_of(core * own_rows, own_rows), own_rows)
    other = pl.ds(pl.multiple_of((1 - core) * own_rows, own_rows), own_rows)
    key_ref[mine, :] = k_ref[...]
    key_ref[other, :] = ko_ref[...]
    wide_ref[mine, 0:128] = v_ref[...]
    wide_ref[other, 0:128] = vo_ref[...]
    wide_ref[:, 128:256] = jnp.ones((2 * own_rows, 128), BF16)
    lse_ref[...] = jnp.zeros(lse_ref.shape, F32)
    copy.wait()
    found = where_ref[3, 0]
    mask = lane_group_mask(per_row, 128)
    factor = scale * LOG2E

    def attend(unit, sub, shifted):
        def one(b, carry):
            row = lax.shift_right_logical(b * unit, 7)
            first = (b * unit) & 127
            entries = [where_ref[row, first + i] for i in range(unit)]
            slots = [e & 255 for e in entries]
            own = [lax.shift_right_logical(s, 3) for s in slots]
            start = [pl.multiple_of((s & 7) * per_row, per_row) for s in slots]
            here = [pl.multiple_of(lax.shift_right_logical(entries[t], 8) * pref, pref) for t in range(0, unit, sub)]
            scores = []
            for t in range(0, unit, sub):
                q = jnp.concatenate([x_ref[own[i], pl.ds(start[i], per_row), :] for i in range(t, t + sub)], axis=0)
                scores.append(
                    lax.dot_general(
                        q, key_ref[pl.ds(here[t // sub], pref), :], (((1,), (1,)), ((), ())), preferred_element_type=F32
                    )
                )
            low, high = carry
            for t in range(0, unit, sub):
                score = scores[t // sub]
                top = jnp.max(score, axis=1, keepdims=True) if shifted else None
                expo = jnp.exp2((score - top if shifted else score) * factor).astype(BF16)
                both = jnp.dot(expo, wide_ref[pl.ds(here[t // sub], pref), :], preferred_element_type=F32)
                total = both[:, 128:256]
                result = (both[:, 0:128] / total).astype(BF16)
                lse = jnp.log(total)
                if shifted:
                    lse = lse + top * scale
                stacked = total.reshape(sub * per_row // 8, 8, 128)
                low = jnp.minimum(low, jnp.min(stacked, axis=0))
                high = jnp.maximum(high, jnp.max(stacked, axis=0))
                for i in range(sub):
                    part = slice(i * per_row, (i + 1) * per_row)
                    out_ref[own[t + i], pl.ds(start[t + i], per_row), :] = result[part]
                    lse_ref[pl.ds(slots[t + i], 1), :] = jnp.sum(
                        jnp.where(mask, lse[part], 0.0), axis=0, keepdims=True
                    )
            return low, high

        return lax.fori_loop(0, (found + unit - 1) // unit, one, (jnp.ones((8, 128), F32), jnp.ones((8, 128), F32)))

    low, high = attend(32, 8, False)
    safe = (jnp.min(low) > 2.0**-70) & (jnp.max(high) < 2.0**100)

    @pl.when(jnp.logical_not(safe))
    def _():
        attend(8, 8, True)

    for s in range(sources):
        full = lse_ref[s * cap:(s + 1) * cap, :]
        high_part = full.astype(BF16).astype(F32)
        rest = full - high_part
        mid_part = rest.astype(BF16).astype(F32)
        low_part = rest - mid_part
        lanes = lax.broadcasted_iota(jnp.int32, full.shape, 1)
        sent = jnp.where(lanes < per_row, high_part, jnp.where(lanes < 2 * per_row, mid_part, low_part))
        out_ref[s, data:data + EXTRA, :] = jnp.concatenate([sent, jnp.zeros_like(sent)], axis=0).astype(BF16)


def merge_kernel(cap, per_row, chunks, place_ref, x_ref, lse_ref, tail_ref, out_ref, sent_ref, weight_ref, done_ref, sems):
    owners = x_ref.shape[0]
    data = cap * per_row
    rows = lse_ref.shape[0]
    batch = rows // chunks
    part = batch * per_row

    def piece(ref, c):
        return ref.at[pl.ds(c * part, part), :]

    stores = [pltpu.make_async_copy(piece(done_ref, c), piece(out_ref, c), sems.at[c]) for c in range(chunks)]
    for o in range(owners):
        sent_ref[o * cap:(o + 1) * cap, :] = x_ref[o, data:data + EXTRA, :].astype(F32)[0:cap, :]
    mask = lane_group_mask(per_row, 128)
    lane = lax.broadcasted_iota(jnp.int32, (batch, 128), 1)
    ones = jnp.ones((128, 128), BF16)
    for c in range(chunks):
        places = [place_ref[0, c * batch + i] for i in range(batch)]
        lse = jnp.concatenate([sent_ref[pl.ds(p, 1), :] for p in places], axis=0)
        terms = jnp.where(lane < 3 * per_row, lse, -lse_ref[c * batch:(c + 1) * batch, :])
        ahead = terms
        for k in range(1, 4):
            ahead = ahead + pltpu.roll(terms, k * per_row, 1)
        weight = 1.0 / (1.0 + jnp.exp(-ahead))
        high = weight.astype(BF16).astype(F32)
        rest = weight - high
        mid = rest.astype(BF16).astype(F32)
        low = jnp.where(lane < 3 * per_row, rest - mid, 0.0)
        weight_ref[c * batch:(c + 1) * batch, :] = jnp.where(lane < per_row, high, jnp.where(lane < 2 * per_row, mid, low))
        spread = jnp.concatenate(
            [jnp.where(mask, weight_ref[c * batch + i:c * batch + i + 1, :], 0.0).astype(BF16) for i in range(batch)], axis=0
        )
        weight_p = jnp.dot(spread, ones, preferred_element_type=F32)
        for i in range(batch):
            here = slice(i * per_row, (i + 1) * per_row)
            there = slice(c * part + i * per_row, c * part + (i + 1) * per_row)
            start = pl.multiple_of((places[i] & 7) * per_row, per_row)
            prefix = x_ref[lax.shift_right_logical(places[i], 3), pl.ds(start, per_row), :].astype(F32)
            tail = tail_ref[there, :]
            done_ref[there, :] = (tail + weight_p[here] * (prefix - tail)).astype(BF16)
        stores[c].start()
    for store in stores:
        store.wait()


def vmem():
    return pl.BlockSpec(memory_space=pltpu.VMEM)


def hbm():
    return pl.BlockSpec(memory_space=pltpu.MemorySpace.HBM)


def in_vmem(x):
    return pltpu.with_memory_space_constraint(x, pltpu.VMEM)


def in_hbm(x):
    return pltpu.with_memory_space_constraint(x, pltpu.HBM)


def smem():
    return pl.BlockSpec(memory_space=pltpu.SMEM)


def body(
    queries, new_keys, new_values, tail_keys, tail_values, prefix_keys, prefix_values, route_owner, group_slot, tail_len
):
    rows, steps, heads, width = queries.shape
    owners = lax.axis_size("roll")
    cap = 8
    per_row = steps * heads
    scale = 1.0 / math.sqrt(width)
    slots = tail_keys.shape[2]
    pref = prefix_keys.shape[2]
    groups = prefix_keys.shape[0]
    block = cap * per_row + EXTRA
    code = (route_owner * 2 + group_slot) * 256 + tail_len
    codes = lax.all_gather(code, "tp", axis=0, tiled=True)
    flat = queries.reshape(rows * per_row, width)

    def params(grant):
        return pltpu.CompilerParams(vmem_limit_bytes=grant * MIB)

    sent, place = pl.pallas_call(
        functools.partial(pack_kernel, cap, per_row),
        out_shape=(
            pltpu.HBM((owners, block, width), BF16),
            jax.ShapeDtypeStruct((1, rows), jnp.int32),
        ),
        in_specs=[vmem(), hbm()],
        out_specs=(hbm(), vmem()),
        scratch_shapes=[
            pltpu.VMEM((rows * per_row, width), BF16),
            pltpu.VMEM((owners, EXTRA, 128), BF16),
            pltpu.SMEM((1, rows), jnp.int32),
            pltpu.SemaphoreType.DMA((3,)),
        ],
        compiler_params=params(8),
        cost_estimate=pl.CostEstimate(flops=0, bytes_accessed=3 * MIB, transcendentals=0),
        name="pack",
    )(codes, in_hbm(flat))
    arrived = lax.all_to_all(sent, "roll", split_axis=0, concat_axis=0, tiled=True)

    batch = 8
    part = batch * per_row
    tail_out, tail_lse = pl.pallas_call(
        functools.partial(tail_kernel, steps, per_row, batch, scale),
        out_shape=(
            pltpu.VMEM((rows * per_row, width), F32),
            pltpu.VMEM((rows, 128), F32),
        ),
        grid=(rows // batch,),
        in_specs=[
            smem(),
            pl.BlockSpec((part, width), lambda i: (i, 0)),
            pl.BlockSpec((batch * slots, width), lambda i: (i, 0)),
            pl.BlockSpec((batch * slots, width), lambda i: (i, 0)),
            pl.BlockSpec((batch * steps, width), lambda i: (i, 0)),
            pl.BlockSpec((batch * steps, width), lambda i: (i, 0)),
        ],
        out_specs=(
            pl.BlockSpec((part, width), lambda i: (i, 0)),
            pl.BlockSpec((batch, 128), lambda i: (i, 0)),
        ),
        compiler_params=params(16),
        cost_estimate=pl.CostEstimate(
            flops=4 * rows * per_row * slots * width, bytes_accessed=12 * MIB, transcendentals=rows * per_row * slots
        ),
        name="tail",
    )(
        codes, in_hbm(flat), in_hbm(tail_keys.reshape(rows * slots, width)), in_hbm(tail_values.reshape(rows * slots, width)),
        new_keys.reshape(rows * steps, width), new_values.reshape(rows * steps, width),
    )

    keys = prefix_keys.reshape(groups * pref, width)
    values = prefix_values.reshape(groups * pref, width)
    pairs = [(i, i ^ 1) for i in range(owners)]
    keys_other = lax.ppermute(keys, "roll", pairs)
    values_other = lax.ppermute(values, "roll", pairs)
    arrived, tail_out, tail_lse = lax.optimization_barrier((arrived, tail_out, tail_lse))
    answered = pl.pallas_call(
        functools.partial(prefix_kernel, cap, per_row, pref, scale),
        out_shape=pltpu.VMEM((owners, block, width), BF16),
        in_specs=[vmem()] * 5,
        out_specs=vmem(),
        scratch_shapes=[
            pltpu.VMEM((2 * groups * pref, width), BF16),
            pltpu.VMEM((2 * groups * pref, 2 * width), BF16),
            pltpu.VMEM((8, 128), jnp.int32),
            pltpu.VMEM((owners * cap, 128), F32),
            pltpu.SMEM((8, 128), jnp.int32),
            pltpu.SemaphoreType.DMA((1,)),
        ],
        compiler_params=params(24),
        cost_estimate=pl.CostEstimate(
            flops=4 * owners * cap * per_row * pref * width, bytes_accessed=6 * MIB,
            transcendentals=owners * cap * per_row * pref,
        ),
        name="prefix",
    )(arrived, keys, values, keys_other, values_other)
    back = lax.all_to_all(answered, "roll", split_axis=0, concat_axis=0, tiled=True)

    chunks = 4
    merged = pl.pallas_call(
        functools.partial(merge_kernel, cap, per_row, chunks),
        out_shape=pltpu.HBM((rows * per_row, width), BF16),
        in_specs=[smem(), vmem(), vmem(), vmem()],
        out_specs=hbm(),
        scratch_shapes=[
            pltpu.VMEM((owners * cap, 128), F32),
            pltpu.VMEM((rows, 128), F32),
            pltpu.VMEM((rows * per_row, width), BF16),
            pltpu.SemaphoreType.DMA((chunks,)),
        ],
        compiler_params=params(12),
        cost_estimate=pl.CostEstimate(flops=0, bytes_accessed=6 * MIB, transcendentals=0),
        name="merge",
    )(place, in_vmem(back), in_vmem(tail_lse), in_vmem(tail_out))
    return merged.reshape(rows, steps, heads, width)


def solution(mesh):
    return jax.shard_map(
        body,
        mesh=mesh,
        in_specs=(
            P("roll", None, "tp", None),
            P("roll", None, "tp", None),
            P("roll", None, "tp", None),
            P("roll", "tp", None, None),
            P("roll", "tp", None, None),
            P("roll", "tp", None, None),
            P("roll", "tp", None, None),
            P("roll", "tp"),
            P("roll", "tp"),
            P("roll", "tp"),
        ),
        out_specs=P("roll", None, "tp", None),
        check_vma=False,
    )
```

```python
import functools
import math

import jax
import jax.numpy as jnp
from jax import lax
from jax.experimental import pallas as pl
from jax.experimental.pallas import tpu as pltpu
from jax.sharding import PartitionSpec as P

LOG2E = math.log2(math.e)
MIB = 1 << 20
F32 = jnp.float32
BF16 = jnp.bfloat16
EXTRA = 8


def lane_group_mask(per_row, width):
    sub = lax.broadcasted_iota(jnp.int32, (per_row, width), 0)
    lane = lax.broadcasted_iota(jnp.int32, (per_row, width), 1)
    return (lane % per_row) == sub


def pack_kernel(cap, per_row, code_ref, q_ref, out_ref, place_ref, held_ref, extra_ref, where_ref, sems):
    lines, line = code_ref.shape
    rows = lines * line
    owners = out_ref.shape[0]
    load = pltpu.make_async_copy(q_ref, held_ref, sems.at[0])
    load.start()
    group = lax.shift_right_logical(code_ref[...], 8).astype(F32).astype(BF16)
    z = lax.broadcasted_iota(jnp.int32, (lines, rows), 0)
    r = lax.broadcasted_iota(jnp.int32, (lines, rows), 1)
    j = lax.broadcasted_iota(jnp.int32, (line, rows), 0)
    rj = lax.broadcasted_iota(jnp.int32, (line, rows), 1)
    spread = jnp.dot(group, (rj % line == j).astype(BF16), preferred_element_type=F32)
    across = jnp.sum(jnp.where(r // line == z, spread, 0.0), axis=0, keepdims=True)
    rz = lax.broadcasted_iota(jnp.int32, (rows, lines), 0)
    zz = lax.broadcasted_iota(jnp.int32, (rows, lines), 1)
    picked = jnp.dot((rz // line == zz).astype(BF16), group, preferred_element_type=F32)
    rl = lax.broadcasted_iota(jnp.int32, (rows, line), 0)
    jl = lax.broadcasted_iota(jnp.int32, (rows, line), 1)
    picked = jnp.where(rl % line == jl, picked, 0.0).astype(BF16)
    down = jnp.dot(picked, jnp.ones((line, rows), BF16), preferred_element_type=F32)
    across = across.astype(jnp.int32)
    down = down.astype(jnp.int32)
    sub = lax.broadcasted_iota(jnp.int32, (rows, rows), 0)
    lane = lax.broadcasted_iota(jnp.int32, (rows, rows), 1)
    chip = lax.shift_right_logical(across, 2)
    shared = lax.shift_right_logical(down, 2) == chip
    before = shared & (down * rows + sub < across * rows + lane)
    rank = jnp.sum(jnp.where(before, 1.0, 0.0), axis=0, keepdims=True).astype(jnp.int32)
    number = jnp.sum(jnp.where(shared, 1.0, 0.0), axis=0, keepdims=True).astype(jnp.int32)
    half = lax.shift_right_logical(number + ((lax.axis_index("roll") + chip) & 1), 1)
    core = (rank >= half).astype(jnp.int32)
    device = chip * 2 + core
    place = device * cap + rank - core * half
    place_ref[...] = place
    index = pltpu.make_async_copy(place_ref, where_ref, sems.at[1])
    index.start()
    named = lax.broadcasted_iota(jnp.int32, (4 * owners, rows), 0) == device * 4 + (across & 3)
    counts = jnp.dot(named.astype(BF16), jnp.ones((rows, 128), BF16), preferred_element_type=F32).astype(BF16)
    ii = lax.broadcasted_iota(jnp.int32, (owners * EXTRA, 4 * owners), 0)
    kk = lax.broadcasted_iota(jnp.int32, (owners * EXTRA, 4 * owners), 1)
    repeat = (lax.shift_right_logical(ii, 1) == kk).astype(BF16)
    extra_ref[...] = jnp.dot(repeat, counts, preferred_element_type=F32).astype(BF16).reshape(owners, EXTRA, 128)
    more = pltpu.make_async_copy(extra_ref, out_ref.at[:, pl.ds(cap * per_row, EXTRA), :], sems.at[2])
    more.start()
    index.wait()
    load.wait()

    def one(i, carry):
        at = where_ref[0, i]
        pltpu.make_async_copy(
            held_ref.at[pl.ds(pl.multiple_of(i * per_row, per_row), per_row), :],
            out_ref.at[lax.shift_right_logical(at, 3), pl.ds(pl.multiple_of((at & 7) * per_row, per_row), per_row), :],
            sems.at[0],
        ).start()
        return carry

    lax.fori_loop(0, rows, one, 0, unroll=16)
    more.wait()
    load.wait()


def tail_kernel(steps, per_row, batch, scale, code_ref, q_ref, tk_ref, tv_ref, nk_ref, nv_ref, out_ref, lse_ref):
    base = pl.program_id(0) * batch
    line = code_ref.shape[1]
    slots = tk_ref.shape[0] // batch
    heads = per_row // steps
    total_rows = batch * per_row
    q = q_ref[...]
    parts = []
    lane = lax.broadcasted_iota(jnp.int32, (per_row, slots), 1)
    for i in range(batch):
        r = base + i
        length = code_ref[r // line, r % line] & 255
        s = lax.dot_general(
            q[i * per_row:(i + 1) * per_row], tk_ref[i * slots:(i + 1) * slots, :],
            (((1,), (1,)), ((), ())), preferred_element_type=F32,
        )
        parts.append(jnp.where(lane < length, s, -jnp.inf))
    st = jnp.concatenate(parts, axis=0)
    sn = lax.dot_general(q, nk_ref[...], (((1,), (1,)), ((), ())), preferred_element_type=F32)
    row = lax.broadcasted_iota(jnp.int32, sn.shape, 0)
    col = lax.broadcasted_iota(jnp.int32, sn.shape, 1)
    own = (row // per_row) == (col // steps)
    causal = (col % steps) <= ((row % per_row) // heads)
    sn = jnp.where(own & causal, sn, -jnp.inf)
    top = jnp.maximum(jnp.max(st, axis=1, keepdims=True), jnp.max(sn, axis=1, keepdims=True))
    et = jnp.exp2((st - top) * (scale * LOG2E))
    en = jnp.exp2((sn - top) * (scale * LOG2E))
    total = jnp.sum(et, axis=1, keepdims=True) + jnp.sum(en, axis=1, keepdims=True)
    pt = et.astype(BF16)
    summed = jnp.concatenate(
        [
            jnp.dot(pt[i * per_row:(i + 1) * per_row], tv_ref[i * slots:(i + 1) * slots, :], preferred_element_type=F32)
            for i in range(batch)
        ],
        axis=0,
    )
    summed = summed + jnp.dot(en.astype(BF16), nv_ref[...], preferred_element_type=F32)
    out_ref[...] = summed / total
    lse = top * scale + jnp.log(total)
    mask = lane_group_mask(per_row, 128)
    for i in range(batch):
        one = jnp.where(mask, lse[i * per_row:(i + 1) * per_row], 0.0)
        lse_ref[i:i + 1, :] = jnp.sum(one, axis=0, keepdims=True)


def prefix_kernel(
    cap, per_row, pref, scale, x_ref, k_ref, v_ref, ko_ref, vo_ref, out_ref, key_ref, wide_ref, list_ref, lse_ref,
    where_ref, sems
):
    sources = x_ref.shape[0]
    data = cap * per_row
    own_rows = k_ref.shape[0]
    i = lax.broadcasted_iota(jnp.int32, (sources, sources), 0)
    j = lax.broadcasted_iota(jnp.int32, (sources, sources), 1)
    lower = (j <= i).astype(BF16)
    source = lax.broadcasted_iota(jnp.int32, (sources, 128), 0).astype(F32)
    lane = lax.broadcasted_iota(jnp.int32, (1, 128), 1).astype(F32)
    tiles = [x_ref[s, data:data + EXTRA, :].astype(F32) for s in range(sources)]
    fore = jnp.zeros((sources, 128), F32)
    end = jnp.zeros((1, 128), F32)
    tables = []
    for g in range(4):
        count = jnp.concatenate([tile[2 * g:2 * g + 1, :] for tile in tiles], axis=0)
        ends = jnp.dot(lower, count.astype(BF16), preferred_element_type=F32)
        total = ends[sources - 1:sources, :]
        tables.append((end, total, ends - count, ends, source * cap + fore))
        fore = fore + count
        end = end + jnp.floor((total + 7.0) * 0.125) * 8.0
    lists = []
    for h in range(3):
        p = jnp.minimum(lane + 128.0 * h, end - 1.0)
        entry = jnp.zeros((1, 128), F32)
        for g, (base, total, begins, ends, first) in enumerate(tables):
            at = jnp.maximum(jnp.minimum(p - base, total - 1.0), 0.0)
            mine = (begins <= at) & (at < ends)
            slot = jnp.sum(jnp.where(mine, first + at - begins, 0.0), axis=0, keepdims=True)
            entry = jnp.where((p >= base) & (total > 0.0), slot + 256.0 * g, entry)
        lists.append(entry)
    list_ref[...] = jnp.concatenate(lists + [end] + lists + [end], axis=0).astype(jnp.int32)
    copy = pltpu.make_async_copy(list_ref, where_ref, sems.at[0])
    copy.start()
    core = lax.axis_index("roll") & 1
    mine = pl.ds(pl.multiple_of(core * own_rows, own_rows), own_rows)
    other = pl.ds(pl.multiple_of((1 - core) * own_rows, own_rows), own_rows)
    key_ref[mine, :] = k_ref[...]
    key_ref[other, :] = ko_ref[...]
    wide_ref[mine, 0:128] = v_ref[...]
    wide_ref[other, 0:128] = vo_ref[...]
    wide_ref[:, 128:256] = jnp.ones((2 * own_rows, 128), BF16)
    lse_ref[...] = jnp.zeros(lse_ref.shape, F32)
    copy.wait()
    found = where_ref[3, 0]
    mask = lane_group_mask(per_row, 128)
    factor = scale * LOG2E

    def attend(unit, sub, shifted, begin, stop, bounds):
        def one(b, carry):
            row = lax.shift_right_logical(begin + b * unit, 7)
            first = (begin + b * unit) & 127
            entries = [where_ref[row, first + i] for i in range(unit)]
            slots = [e & 255 for e in entries]
            own = [lax.shift_right_logical(s, 3) for s in slots]
            start = [pl.multiple_of((s & 7) * per_row, per_row) for s in slots]
            here = [pl.multiple_of(lax.shift_right_logical(entries[t], 8) * pref, pref) for t in range(0, unit, sub)]
            scores = []
            for t in range(0, unit, sub):
                q = jnp.concatenate([x_ref[own[i], pl.ds(start[i], per_row), :] for i in range(t, t + sub)], axis=0)
                scores.append(
                    lax.dot_general(
                        q, key_ref[pl.ds(here[t // sub], pref), :], (((1,), (1,)), ((), ())), preferred_element_type=F32
                    )
                )
            low, high = carry
            for t in range(0, unit, sub):
                score = scores[t // sub]
                top = jnp.max(score, axis=1, keepdims=True) if shifted else None
                expo = jnp.exp2((score - top if shifted else score) * factor).astype(BF16)
                both = jnp.dot(expo, wide_ref[pl.ds(here[t // sub], pref), :], preferred_element_type=F32)
                total = both[:, 128:256]
                result = (both[:, 0:128] / total).astype(BF16)
                lse = jnp.log(total)
                if shifted:
                    lse = lse + top * scale
                stacked = total.reshape(sub * per_row // 8, 8, 128)
                low = jnp.minimum(low, jnp.min(stacked, axis=0))
                high = jnp.maximum(high, jnp.max(stacked, axis=0))
                for i in range(sub):
                    part = slice(i * per_row, (i + 1) * per_row)
                    out_ref[own[t + i], pl.ds(start[t + i], per_row), :] = result[part]
                    lse_ref[pl.ds(slots[t + i], 1), :] = jnp.sum(
                        jnp.where(mask, lse[part], 0.0), axis=0, keepdims=True
                    )
            return low, high

        return lax.fori_loop(0, lax.shift_right_logical(stop - begin + unit - 1, unit.bit_length() - 1), one, bounds)

    bounds = (jnp.ones((8, 128), F32), jnp.ones((8, 128), F32))
    most = lax.shift_left(lax.shift_right_logical(found + 8, 5), 5)
    bounds = attend(32, 8, False, 0, most, bounds)
    low, high = attend(16, 8, False, most, found, bounds)
    safe = (jnp.min(low) > 2.0**-70) & (jnp.max(high) < 2.0**100)

    @pl.when(jnp.logical_not(safe))
    def _():
        attend(8, 8, True, 0, found, bounds)

    for s in range(sources):
        full = lse_ref[s * cap:(s + 1) * cap, :]
        high_part = full.astype(BF16).astype(F32)
        rest = full - high_part
        mid_part = rest.astype(BF16).astype(F32)
        low_part = rest - mid_part
        lanes = lax.broadcasted_iota(jnp.int32, full.shape, 1)
        sent = jnp.where(lanes < per_row, high_part, jnp.where(lanes < 2 * per_row, mid_part, low_part))
        out_ref[s, data:data + EXTRA, :] = sent.astype(BF16)


def merge_kernel(cap, per_row, chunks, place_ref, x_ref, lse_ref, tail_ref, out_ref, sent_ref, weight_ref, done_ref, sems):
    owners = x_ref.shape[0]
    data = cap * per_row
    rows = lse_ref.shape[0]
    batch = rows // chunks
    part = batch * per_row

    def piece(ref, c):
        return ref.at[pl.ds(c * part, part), :]

    stores = [pltpu.make_async_copy(piece(done_ref, c), piece(out_ref, c), sems.at[c]) for c in range(chunks)]
    for o in range(owners):
        sent_ref[o * cap:(o + 1) * cap, :] = x_ref[o, data:data + EXTRA, :].astype(F32)[0:cap, :]
    mask = lane_group_mask(per_row, 128)
    lane = lax.broadcasted_iota(jnp.int32, (batch, 128), 1)
    ones = jnp.ones((128, 128), BF16)
    for c in range(chunks):
        places = [place_ref[0, c * batch + i] for i in range(batch)]
        lse = jnp.concatenate([sent_ref[pl.ds(p, 1), :] for p in places], axis=0)
        terms = jnp.where(lane < 3 * per_row, lse, -lse_ref[c * batch:(c + 1) * batch, :])
        ahead = terms
        for k in range(1, 4):
            ahead = ahead + pltpu.roll(terms, k * per_row, 1)
        weight = 1.0 / (1.0 + jnp.exp(-ahead))
        high = weight.astype(BF16).astype(F32)
        rest = weight - high
        mid = rest.astype(BF16).astype(F32)
        low = jnp.where(lane < 3 * per_row, rest - mid, 0.0)
        weight_ref[c * batch:(c + 1) * batch, :] = jnp.where(lane < per_row, high, jnp.where(lane < 2 * per_row, mid, low))
        spread = jnp.concatenate(
            [jnp.where(mask, weight_ref[c * batch + i:c * batch + i + 1, :], 0.0).astype(BF16) for i in range(batch)], axis=0
        )
        weight_p = jnp.dot(spread, ones, preferred_element_type=F32)
        for i in range(batch):
            here = slice(i * per_row, (i + 1) * per_row)
            there = slice(c * part + i * per_row, c * part + (i + 1) * per_row)
            start = pl.multiple_of((places[i] & 7) * per_row, per_row)
            prefix = x_ref[lax.shift_right_logical(places[i], 3), pl.ds(start, per_row), :].astype(F32)
            tail = tail_ref[there, :]
            done_ref[there, :] = (tail + weight_p[here] * (prefix - tail)).astype(BF16)
        stores[c].start()
    for store in stores:
        store.wait()


def vmem():
    return pl.BlockSpec(memory_space=pltpu.VMEM)


def hbm():
    return pl.BlockSpec(memory_space=pltpu.MemorySpace.HBM)


def in_vmem(x):
    return pltpu.with_memory_space_constraint(x, pltpu.VMEM)


def in_hbm(x):
    return pltpu.with_memory_space_constraint(x, pltpu.HBM)


def smem():
    return pl.BlockSpec(memory_space=pltpu.SMEM)


def body(
    queries, new_keys, new_values, tail_keys, tail_values, prefix_keys, prefix_values, route_owner, group_slot, tail_len
):
    rows, steps, heads, width = queries.shape
    owners = lax.axis_size("roll")
    cap = 8
    per_row = steps * heads
    scale = 1.0 / math.sqrt(width)
    slots = tail_keys.shape[2]
    pref = prefix_keys.shape[2]
    groups = prefix_keys.shape[0]
    block = cap * per_row + EXTRA
    code = (route_owner * 2 + group_slot) * 256 + tail_len
    lines = lax.axis_size("tp")
    codes = lax.all_to_all(jnp.broadcast_to(code, (lines, code.shape[1])), "tp", split_axis=0, concat_axis=0, tiled=True)
    flat = queries.reshape(rows * per_row, width)

    def params(grant):
        return pltpu.CompilerParams(vmem_limit_bytes=grant * MIB)

    sent, place = pl.pallas_call(
        functools.partial(pack_kernel, cap, per_row),
        out_shape=(
            pltpu.HBM((owners, block, width), BF16),
            jax.ShapeDtypeStruct((1, rows), jnp.int32),
        ),
        in_specs=[vmem(), hbm()],
        out_specs=(hbm(), vmem()),
        scratch_shapes=[
            pltpu.VMEM((rows * per_row, width), BF16),
            pltpu.VMEM((owners, EXTRA, 128), BF16),
            pltpu.SMEM((1, rows), jnp.int32),
            pltpu.SemaphoreType.DMA((3,)),
        ],
        compiler_params=params(8),
        cost_estimate=pl.CostEstimate(flops=0, bytes_accessed=3 * MIB, transcendentals=0),
        name="pack",
    )(codes, in_hbm(flat))
    arrived = lax.all_to_all(sent, "roll", split_axis=0, concat_axis=0, tiled=True)

    batch = 8
    part = batch * per_row
    tail_out, tail_lse = pl.pallas_call(
        functools.partial(tail_kernel, steps, per_row, batch, scale),
        out_shape=(
            pltpu.VMEM((rows * per_row, width), F32),
            pltpu.VMEM((rows, 128), F32),
        ),
        grid=(rows // batch,),
        in_specs=[
            smem(),
            pl.BlockSpec((part, width), lambda i: (i, 0)),
            pl.BlockSpec((batch * slots, width), lambda i: (i, 0)),
            pl.BlockSpec((batch * slots, width), lambda i: (i, 0)),
            pl.BlockSpec((batch * steps, width), lambda i: (i, 0)),
            pl.BlockSpec((batch * steps, width), lambda i: (i, 0)),
        ],
        out_specs=(
            pl.BlockSpec((part, width), lambda i: (i, 0)),
            pl.BlockSpec((batch, 128), lambda i: (i, 0)),
        ),
        compiler_params=params(16),
        cost_estimate=pl.CostEstimate(
            flops=4 * rows * per_row * slots * width, bytes_accessed=12 * MIB, transcendentals=rows * per_row * slots
        ),
        name="tail",
    )(
        codes, in_hbm(flat), in_hbm(tail_keys.reshape(rows * slots, width)), in_hbm(tail_values.reshape(rows * slots, width)),
        new_keys.reshape(rows * steps, width), new_values.reshape(rows * steps, width),
    )

    keys = prefix_keys.reshape(groups * pref, width)
    values = prefix_values.reshape(groups * pref, width)
    pairs = [(i, i ^ 1) for i in range(owners)]
    keys_other = lax.ppermute(keys, "roll", pairs)
    values_other = lax.ppermute(values, "roll", pairs)
    arrived, tail_out, tail_lse = lax.optimization_barrier((arrived, tail_out, tail_lse))
    answered = pl.pallas_call(
        functools.partial(prefix_kernel, cap, per_row, pref, scale),
        out_shape=pltpu.VMEM((owners, block, width), BF16),
        in_specs=[vmem()] * 5,
        out_specs=vmem(),
        scratch_shapes=[
            pltpu.VMEM((2 * groups * pref, width), BF16),
            pltpu.VMEM((2 * groups * pref, 2 * width), BF16),
            pltpu.VMEM((8, 128), jnp.int32),
            pltpu.VMEM((owners * cap, 128), F32),
            pltpu.SMEM((8, 128), jnp.int32),
            pltpu.SemaphoreType.DMA((1,)),
        ],
        compiler_params=params(24),
        cost_estimate=pl.CostEstimate(
            flops=4 * owners * cap * per_row * pref * width, bytes_accessed=6 * MIB,
            transcendentals=owners * cap * per_row * pref,
        ),
        name="prefix",
    )(arrived, keys, values, keys_other, values_other)
    back = lax.all_to_all(answered, "roll", split_axis=0, concat_axis=0, tiled=True)

    chunks = 4
    merged = pl.pallas_call(
        functools.partial(merge_kernel, cap, per_row, chunks),
        out_shape=pltpu.HBM((rows * per_row, width), BF16),
        in_specs=[smem(), vmem(), vmem(), vmem()],
        out_specs=hbm(),
        scratch_shapes=[
            pltpu.VMEM((owners * cap, 128), F32),
            pltpu.VMEM((rows, 128), F32),
            pltpu.VMEM((rows * per_row, width), BF16),
            pltpu.SemaphoreType.DMA((chunks,)),
        ],
        compiler_params=params(12),
        cost_estimate=pl.CostEstimate(flops=0, bytes_accessed=6 * MIB, transcendentals=0),
        name="merge",
    )(place, in_vmem(back), in_vmem(tail_lse), in_vmem(tail_out))
    return merged.reshape(rows, steps, heads, width)


def solution(mesh):
    return jax.shard_map(
        body,
        mesh=mesh,
        in_specs=(
            P("roll", None, "tp", None),
            P("roll", None, "tp", None),
            P("roll", None, "tp", None),
            P("roll", "tp", None, None),
            P("roll", "tp", None, None),
            P("roll", "tp", None, None),
            P("roll", "tp", None, None),
            P("roll", "tp"),
            P("roll", "tp"),
            P("roll", "tp"),
        ),
        out_specs=P("roll", None, "tp", None),
        check_vma=False,
    )
```

```python
import functools
import math

import jax
import jax.numpy as jnp
from jax import lax
from jax.experimental import pallas as pl
from jax.experimental.pallas import tpu as pltpu
from jax.sharding import PartitionSpec as P

LOG2E = math.log2(math.e)
MIB = 1 << 20
F32 = jnp.float32
BF16 = jnp.bfloat16
EXTRA = 8


def lane_group_mask(per_row, width):
    sub = lax.broadcasted_iota(jnp.int32, (per_row, width), 0)
    lane = lax.broadcasted_iota(jnp.int32, (per_row, width), 1)
    return (lane % per_row) == sub


def pack_kernel(cap, per_row, code_ref, q_ref, out_ref, place_ref, held_ref, extra_ref, where_ref, sems):
    lines, line = code_ref.shape
    rows = lines * line
    owners = out_ref.shape[0]
    load = pltpu.make_async_copy(q_ref, held_ref, sems.at[0])
    load.start()
    group = lax.shift_right_logical(code_ref[...], 8).astype(F32).astype(BF16)
    z = lax.broadcasted_iota(jnp.int32, (lines, rows), 0)
    r = lax.broadcasted_iota(jnp.int32, (lines, rows), 1)
    j = lax.broadcasted_iota(jnp.int32, (line, rows), 0)
    rj = lax.broadcasted_iota(jnp.int32, (line, rows), 1)
    spread = jnp.dot(group, (rj % line == j).astype(BF16), preferred_element_type=F32)
    across = jnp.sum(jnp.where(r // line == z, spread, 0.0), axis=0, keepdims=True)
    rz = lax.broadcasted_iota(jnp.int32, (rows, lines), 0)
    zz = lax.broadcasted_iota(jnp.int32, (rows, lines), 1)
    picked = jnp.dot((rz // line == zz).astype(BF16), group, preferred_element_type=F32)
    rl = lax.broadcasted_iota(jnp.int32, (rows, line), 0)
    jl = lax.broadcasted_iota(jnp.int32, (rows, line), 1)
    picked = jnp.where(rl % line == jl, picked, 0.0).astype(BF16)
    down = jnp.dot(picked, jnp.ones((line, rows), BF16), preferred_element_type=F32)
    across = across.astype(jnp.int32)
    down = down.astype(jnp.int32)
    sub = lax.broadcasted_iota(jnp.int32, (rows, rows), 0)
    lane = lax.broadcasted_iota(jnp.int32, (rows, rows), 1)
    chip = lax.shift_right_logical(across, 2)
    shared = lax.shift_right_logical(down, 2) == chip
    before = shared & (down * rows + sub < across * rows + lane)
    rank = jnp.sum(jnp.where(before, 1.0, 0.0), axis=0, keepdims=True).astype(jnp.int32)
    number = jnp.sum(jnp.where(shared, 1.0, 0.0), axis=0, keepdims=True).astype(jnp.int32)
    half = lax.shift_right_logical(number + ((lax.axis_index("roll") + chip) & 1), 1)
    core = (rank >= half).astype(jnp.int32)
    device = chip * 2 + core
    place = device * cap + rank - core * half
    place_ref[...] = place
    index = pltpu.make_async_copy(place_ref, where_ref, sems.at[1])
    index.start()
    named = lax.broadcasted_iota(jnp.int32, (4 * owners, rows), 0) == device * 4 + (across & 3)
    counts = jnp.dot(named.astype(BF16), jnp.ones((rows, 128), BF16), preferred_element_type=F32).astype(BF16)
    ii = lax.broadcasted_iota(jnp.int32, (owners * EXTRA, 4 * owners), 0)
    kk = lax.broadcasted_iota(jnp.int32, (owners * EXTRA, 4 * owners), 1)
    repeat = (lax.shift_right_logical(ii, 1) == kk).astype(BF16)
    extra_ref[...] = jnp.dot(repeat, counts, preferred_element_type=F32).astype(BF16).reshape(owners, EXTRA, 128)
    more = pltpu.make_async_copy(extra_ref, out_ref.at[:, pl.ds(cap * per_row, EXTRA), :], sems.at[2])
    more.start()
    index.wait()
    load.wait()

    def one(i, carry):
        at = where_ref[0, i]
        pltpu.make_async_copy(
            held_ref.at[pl.ds(pl.multiple_of(i * per_row, per_row), per_row), :],
            out_ref.at[lax.shift_right_logical(at, 3), pl.ds(pl.multiple_of((at & 7) * per_row, per_row), per_row), :],
            sems.at[0],
        ).start()
        return carry

    lax.fori_loop(0, rows, one, 0, unroll=16)
    more.wait()
    load.wait()


def tail_kernel(steps, per_row, batch, scale, code_ref, q_ref, tk_ref, tv_ref, nk_ref, nv_ref, out_ref, lse_ref):
    base = pl.program_id(0) * batch
    line = code_ref.shape[1]
    slots = tk_ref.shape[0] // batch
    heads = per_row // steps
    total_rows = batch * per_row
    q = q_ref[...]
    parts = []
    lane = lax.broadcasted_iota(jnp.int32, (per_row, slots), 1)
    for i in range(batch):
        r = base + i
        length = code_ref[r // line, r % line] & 255
        s = lax.dot_general(
            q[i * per_row:(i + 1) * per_row], tk_ref[i * slots:(i + 1) * slots, :],
            (((1,), (1,)), ((), ())), preferred_element_type=F32,
        )
        parts.append(jnp.where(lane < length, s, -jnp.inf))
    st = jnp.concatenate(parts, axis=0)
    sn = lax.dot_general(q, nk_ref[...], (((1,), (1,)), ((), ())), preferred_element_type=F32)
    row = lax.broadcasted_iota(jnp.int32, sn.shape, 0)
    col = lax.broadcasted_iota(jnp.int32, sn.shape, 1)
    own = (row // per_row) == (col // steps)
    causal = (col % steps) <= ((row % per_row) // heads)
    sn = jnp.where(own & causal, sn, -jnp.inf)
    top = jnp.maximum(jnp.max(st, axis=1, keepdims=True), jnp.max(sn, axis=1, keepdims=True))
    et = jnp.exp2((st - top) * (scale * LOG2E))
    en = jnp.exp2((sn - top) * (scale * LOG2E))
    total = jnp.sum(et, axis=1, keepdims=True) + jnp.sum(en, axis=1, keepdims=True)
    pt = et.astype(BF16)
    summed = jnp.concatenate(
        [
            jnp.dot(pt[i * per_row:(i + 1) * per_row], tv_ref[i * slots:(i + 1) * slots, :], preferred_element_type=F32)
            for i in range(batch)
        ],
        axis=0,
    )
    summed = summed + jnp.dot(en.astype(BF16), nv_ref[...], preferred_element_type=F32)
    out_ref[...] = summed / total
    lse = top * scale + jnp.log(total)
    mask = lane_group_mask(per_row, 128)
    for i in range(batch):
        one = jnp.where(mask, lse[i * per_row:(i + 1) * per_row], 0.0)
        lse_ref[i:i + 1, :] = jnp.sum(one, axis=0, keepdims=True)


def prefix_kernel(
    cap, per_row, pref, scale, x_ref, k_ref, v_ref, ko_ref, vo_ref, out_ref, key_ref, wide_ref, list_ref, lse_ref,
    where_ref, sems
):
    sources = x_ref.shape[0]
    data = cap * per_row
    own_rows = k_ref.shape[0]
    core = lax.axis_index("roll") & 1
    kept = pl.ds(pl.multiple_of(core * own_rows, own_rows), own_rows)
    other = pl.ds(pl.multiple_of((1 - core) * own_rows, own_rows), own_rows)
    loads = [
        pltpu.make_async_copy(ko_ref, key_ref.at[other, :], sems.at[1]),
        pltpu.make_async_copy(vo_ref, wide_ref.at[other, pl.ds(0, 128)], sems.at[2]),
    ]
    for load in loads:
        load.start()
    i = lax.broadcasted_iota(jnp.int32, (sources, sources), 0)
    j = lax.broadcasted_iota(jnp.int32, (sources, sources), 1)
    lower = (j <= i).astype(BF16)
    source = lax.broadcasted_iota(jnp.int32, (sources, 128), 0).astype(F32)
    lane = lax.broadcasted_iota(jnp.int32, (1, 128), 1).astype(F32)
    tiles = [x_ref[s, data:data + EXTRA, :].astype(F32) for s in range(sources)]
    fore = jnp.zeros((sources, 128), F32)
    end = jnp.zeros((1, 128), F32)
    tables = []
    for g in range(4):
        count = jnp.concatenate([tile[2 * g:2 * g + 1, :] for tile in tiles], axis=0)
        ends = jnp.dot(lower, count.astype(BF16), preferred_element_type=F32)
        total = ends[sources - 1:sources, :]
        tables.append((end, total, ends - count, ends, source * cap + fore))
        fore = fore + count
        end = end + jnp.floor((total + 7.0) * 0.125) * 8.0
    lists = []
    for h in range(3):
        p = jnp.minimum(lane + 128.0 * h, end - 1.0)
        entry = jnp.zeros((1, 128), F32)
        for g, (base, total, begins, ends, first) in enumerate(tables):
            at = jnp.maximum(jnp.minimum(p - base, total - 1.0), 0.0)
            mine = (begins <= at) & (at < ends)
            slot = jnp.sum(jnp.where(mine, first + at - begins, 0.0), axis=0, keepdims=True)
            entry = jnp.where((p >= base) & (total > 0.0), slot + 256.0 * g, entry)
        lists.append(entry)
    list_ref[...] = jnp.concatenate(lists + [end] + lists + [end], axis=0).astype(jnp.int32)
    copy = pltpu.make_async_copy(list_ref, where_ref, sems.at[0])
    copy.start()
    key_ref[kept, :] = k_ref[...]
    wide_ref[kept, 0:128] = v_ref[...]
    wide_ref[:, 128:256] = jnp.ones((2 * own_rows, 128), BF16)
    lse_ref[...] = jnp.zeros(lse_ref.shape, F32)
    copy.wait()
    found = where_ref[3, 0]
    for load in loads:
        load.wait()
    mask = lane_group_mask(per_row, 128)
    factor = scale * LOG2E

    def attend(unit, sub, shifted, begin, stop, bounds):
        def one(b, carry):
            row = lax.shift_right_logical(begin + b * unit, 7)
            first = (begin + b * unit) & 127
            entries = [where_ref[row, first + i] for i in range(unit)]
            slots = [e & 255 for e in entries]
            own = [lax.shift_right_logical(s, 3) for s in slots]
            start = [pl.multiple_of((s & 7) * per_row, per_row) for s in slots]
            here = [pl.multiple_of(lax.shift_right_logical(entries[t], 8) * pref, pref) for t in range(0, unit, sub)]
            scores = []
            for t in range(0, unit, sub):
                q = jnp.concatenate([x_ref[own[i], pl.ds(start[i], per_row), :] for i in range(t, t + sub)], axis=0)
                scores.append(
                    lax.dot_general(
                        q, key_ref[pl.ds(here[t // sub], pref), :], (((1,), (1,)), ((), ())), preferred_element_type=F32
                    )
                )
            low, high = carry
            for t in range(0, unit, sub):
                score = scores[t // sub]
                top = jnp.max(score, axis=1, keepdims=True) if shifted else None
                expo = jnp.exp2((score - top if shifted else score) * factor).astype(BF16)
                both = jnp.dot(expo, wide_ref[pl.ds(here[t // sub], pref), :], preferred_element_type=F32)
                total = both[:, 128:256]
                result = (both[:, 0:128] / total).astype(BF16)
                lse = jnp.log(total)
                if shifted:
                    lse = lse + top * scale
                stacked = total.reshape(sub * per_row // 8, 8, 128)
                low = jnp.minimum(low, jnp.min(stacked, axis=0))
                high = jnp.maximum(high, jnp.max(stacked, axis=0))
                for i in range(sub):
                    part = slice(i * per_row, (i + 1) * per_row)
                    out_ref[own[t + i], pl.ds(start[t + i], per_row), :] = result[part]
                    lse_ref[pl.ds(slots[t + i], 1), :] = jnp.sum(
                        jnp.where(mask, lse[part], 0.0), axis=0, keepdims=True
                    )
            return low, high

        return lax.fori_loop(0, lax.shift_right_logical(stop - begin + unit - 1, unit.bit_length() - 1), one, bounds)

    bounds = (jnp.ones((8, 128), F32), jnp.ones((8, 128), F32))
    long = lax.shift_left(lax.shift_right_logical(found, 6), 6)
    most = lax.shift_left(lax.shift_right_logical(found + 8, 5), 5)
    bounds = attend(64, 8, False, 0, long, bounds)
    bounds = attend(32, 8, False, long, most, bounds)
    low, high = attend(16, 8, False, most, found, bounds)
    safe = (jnp.min(low) > 2.0**-70) & (jnp.max(high) < 2.0**100)

    @pl.when(jnp.logical_not(safe))
    def _():
        attend(8, 8, True, 0, found, bounds)

    for s in range(sources):
        full = lse_ref[s * cap:(s + 1) * cap, :]
        high_part = full.astype(BF16).astype(F32)
        rest = full - high_part
        mid_part = rest.astype(BF16).astype(F32)
        low_part = rest - mid_part
        lanes = lax.broadcasted_iota(jnp.int32, full.shape, 1)
        sent = jnp.where(lanes < per_row, high_part, jnp.where(lanes < 2 * per_row, mid_part, low_part))
        out_ref[s, data:data + EXTRA, :] = sent.astype(BF16)


def merge_kernel(cap, per_row, chunks, place_ref, x_ref, lse_ref, tail_ref, out_ref, sent_ref, weight_ref, done_ref, sems):
    owners = x_ref.shape[0]
    data = cap * per_row
    rows = lse_ref.shape[0]
    batch = rows // chunks
    part = batch * per_row

    def piece(ref, c):
        return ref.at[pl.ds(c * part, part), :]

    stores = [pltpu.make_async_copy(piece(done_ref, c), piece(out_ref, c), sems.at[c]) for c in range(chunks)]
    for o in range(owners):
        sent_ref[o * cap:(o + 1) * cap, :] = x_ref[o, data:data + EXTRA, :].astype(F32)[0:cap, :]
    mask = lane_group_mask(per_row, 128)
    lane = lax.broadcasted_iota(jnp.int32, (batch, 128), 1)
    ones = jnp.ones((128, 128), BF16)
    for c in range(chunks):
        places = [place_ref[0, c * batch + i] for i in range(batch)]
        lse = jnp.concatenate([sent_ref[pl.ds(p, 1), :] for p in places], axis=0)
        terms = jnp.where(lane < 3 * per_row, lse, -lse_ref[c * batch:(c + 1) * batch, :])
        ahead = terms
        for k in range(1, 4):
            ahead = ahead + pltpu.roll(terms, k * per_row, 1)
        weight = 1.0 / (1.0 + jnp.exp(-ahead))
        high = weight.astype(BF16).astype(F32)
        rest = weight - high
        mid = rest.astype(BF16).astype(F32)
        low = jnp.where(lane < 3 * per_row, rest - mid, 0.0)
        weight_ref[c * batch:(c + 1) * batch, :] = jnp.where(lane < per_row, high, jnp.where(lane < 2 * per_row, mid, low))
        spread = jnp.concatenate(
            [jnp.where(mask, weight_ref[c * batch + i:c * batch + i + 1, :], 0.0).astype(BF16) for i in range(batch)], axis=0
        )
        weight_p = jnp.dot(spread, ones, preferred_element_type=F32)
        for i in range(batch):
            here = slice(i * per_row, (i + 1) * per_row)
            there = slice(c * part + i * per_row, c * part + (i + 1) * per_row)
            start = pl.multiple_of((places[i] & 7) * per_row, per_row)
            prefix = x_ref[lax.shift_right_logical(places[i], 3), pl.ds(start, per_row), :].astype(F32)
            tail = tail_ref[there, :]
            done_ref[there, :] = (tail + weight_p[here] * (prefix - tail)).astype(BF16)
        stores[c].start()
    for store in stores:
        store.wait()


def vmem():
    return pl.BlockSpec(memory_space=pltpu.VMEM)


def hbm():
    return pl.BlockSpec(memory_space=pltpu.MemorySpace.HBM)


def in_vmem(x):
    return pltpu.with_memory_space_constraint(x, pltpu.VMEM)


def in_hbm(x):
    return pltpu.with_memory_space_constraint(x, pltpu.HBM)


def smem():
    return pl.BlockSpec(memory_space=pltpu.SMEM)


def body(
    queries, new_keys, new_values, tail_keys, tail_values, prefix_keys, prefix_values, route_owner, group_slot, tail_len
):
    rows, steps, heads, width = queries.shape
    owners = lax.axis_size("roll")
    cap = 8
    per_row = steps * heads
    scale = 1.0 / math.sqrt(width)
    slots = tail_keys.shape[2]
    pref = prefix_keys.shape[2]
    groups = prefix_keys.shape[0]
    block = cap * per_row + EXTRA
    code = (route_owner * 2 + group_slot) * 256 + tail_len
    lines = lax.axis_size("tp")
    codes = lax.all_to_all(jnp.broadcast_to(code, (lines, code.shape[1])), "tp", split_axis=0, concat_axis=0, tiled=True)
    flat = queries.reshape(rows * per_row, width)

    def params(grant):
        return pltpu.CompilerParams(vmem_limit_bytes=grant * MIB)

    sent, place = pl.pallas_call(
        functools.partial(pack_kernel, cap, per_row),
        out_shape=(
            pltpu.HBM((owners, block, width), BF16),
            jax.ShapeDtypeStruct((1, rows), jnp.int32),
        ),
        in_specs=[vmem(), hbm()],
        out_specs=(hbm(), vmem()),
        scratch_shapes=[
            pltpu.VMEM((rows * per_row, width), BF16),
            pltpu.VMEM((owners, EXTRA, 128), BF16),
            pltpu.SMEM((1, rows), jnp.int32),
            pltpu.SemaphoreType.DMA((3,)),
        ],
        compiler_params=params(8),
        cost_estimate=pl.CostEstimate(flops=0, bytes_accessed=3 * MIB, transcendentals=0),
        name="pack",
    )(codes, in_hbm(flat))
    arrived = lax.all_to_all(sent, "roll", split_axis=0, concat_axis=0, tiled=True)

    batch = 8
    part = batch * per_row
    tail_out, tail_lse = pl.pallas_call(
        functools.partial(tail_kernel, steps, per_row, batch, scale),
        out_shape=(
            pltpu.VMEM((rows * per_row, width), F32),
            pltpu.VMEM((rows, 128), F32),
        ),
        grid=(rows // batch,),
        in_specs=[
            smem(),
            pl.BlockSpec((part, width), lambda i: (i, 0)),
            pl.BlockSpec((batch * slots, width), lambda i: (i, 0)),
            pl.BlockSpec((batch * slots, width), lambda i: (i, 0)),
            pl.BlockSpec((batch * steps, width), lambda i: (i, 0)),
            pl.BlockSpec((batch * steps, width), lambda i: (i, 0)),
        ],
        out_specs=(
            pl.BlockSpec((part, width), lambda i: (i, 0)),
            pl.BlockSpec((batch, 128), lambda i: (i, 0)),
        ),
        compiler_params=params(16),
        cost_estimate=pl.CostEstimate(
            flops=4 * rows * per_row * slots * width, bytes_accessed=12 * MIB, transcendentals=rows * per_row * slots
        ),
        name="tail",
    )(
        codes, in_hbm(flat), in_hbm(tail_keys.reshape(rows * slots, width)), in_hbm(tail_values.reshape(rows * slots, width)),
        new_keys.reshape(rows * steps, width), new_values.reshape(rows * steps, width),
    )

    keys = prefix_keys.reshape(groups * pref, width)
    values = prefix_values.reshape(groups * pref, width)
    pairs = [(i, i ^ 1) for i in range(owners)]
    keys_other = lax.ppermute(keys, "roll", pairs)
    values_other = lax.ppermute(values, "roll", pairs)
    arrived, tail_out, tail_lse = lax.optimization_barrier((arrived, tail_out, tail_lse))
    answered = pl.pallas_call(
        functools.partial(prefix_kernel, cap, per_row, pref, scale),
        out_shape=pltpu.VMEM((owners, block, width), BF16),
        in_specs=[vmem()] * 3 + [hbm()] * 2,
        out_specs=vmem(),
        scratch_shapes=[
            pltpu.VMEM((2 * groups * pref, width), BF16),
            pltpu.VMEM((2 * groups * pref, 2 * width), BF16),
            pltpu.VMEM((8, 128), jnp.int32),
            pltpu.VMEM((owners * cap, 128), F32),
            pltpu.SMEM((8, 128), jnp.int32),
            pltpu.SemaphoreType.DMA((3,)),
        ],
        compiler_params=params(24),
        cost_estimate=pl.CostEstimate(
            flops=4 * owners * cap * per_row * pref * width, bytes_accessed=6 * MIB,
            transcendentals=owners * cap * per_row * pref,
        ),
        name="prefix",
    )(arrived, in_vmem(keys), in_vmem(values), in_hbm(keys_other), in_hbm(values_other))
    back = lax.all_to_all(answered, "roll", split_axis=0, concat_axis=0, tiled=True)

    chunks = 4
    merged = pl.pallas_call(
        functools.partial(merge_kernel, cap, per_row, chunks),
        out_shape=pltpu.HBM((rows * per_row, width), BF16),
        in_specs=[smem(), vmem(), vmem(), vmem()],
        out_specs=hbm(),
        scratch_shapes=[
            pltpu.VMEM((owners * cap, 128), F32),
            pltpu.VMEM((rows, 128), F32),
            pltpu.VMEM((rows * per_row, width), BF16),
            pltpu.SemaphoreType.DMA((chunks,)),
        ],
        compiler_params=params(12),
        cost_estimate=pl.CostEstimate(flops=0, bytes_accessed=6 * MIB, transcendentals=0),
        name="merge",
    )(place, in_vmem(back), in_vmem(tail_lse), in_vmem(tail_out))
    return merged.reshape(rows, steps, heads, width)


def solution(mesh):
    return jax.shard_map(
        body,
        mesh=mesh,
        in_specs=(
            P("roll", None, "tp", None),
            P("roll", None, "tp", None),
            P("roll", None, "tp", None),
            P("roll", "tp", None, None),
            P("roll", "tp", None, None),
            P("roll", "tp", None, None),
            P("roll", "tp", None, None),
            P("roll", "tp"),
            P("roll", "tp"),
            P("roll", "tp"),
        ),
        out_specs=P("roll", None, "tp", None),
        check_vma=False,
    )
```

```python
import functools
import math

import jax
import jax.numpy as jnp
from jax import lax
from jax.experimental import pallas as pl
from jax.experimental.pallas import tpu as pltpu
from jax.sharding import PartitionSpec as P

LOG2E = math.log2(math.e)
MIB = 1 << 20
F32 = jnp.float32
BF16 = jnp.bfloat16
EXTRA = 16
BACK = 8


def lane_group_mask(per_row, width):
    sub = lax.broadcasted_iota(jnp.int32, (per_row, width), 0)
    lane = lax.broadcasted_iota(jnp.int32, (per_row, width), 1)
    return (lane % per_row) == sub


def pack_kernel(cap, per_row, code_ref, q_ref, out_ref, place_ref, held_ref, extra_ref, where_ref, sems):
    lines, line = code_ref.shape
    rows = lines * line
    owners = out_ref.shape[0]
    load = pltpu.make_async_copy(q_ref, held_ref, sems.at[0])
    load.start()
    group = lax.shift_right_logical(code_ref[...], 8).astype(F32).astype(BF16)
    z = lax.broadcasted_iota(jnp.int32, (lines, rows), 0)
    r = lax.broadcasted_iota(jnp.int32, (lines, rows), 1)
    j = lax.broadcasted_iota(jnp.int32, (line, rows), 0)
    rj = lax.broadcasted_iota(jnp.int32, (line, rows), 1)
    spread = jnp.dot(group, (rj % line == j).astype(BF16), preferred_element_type=F32)
    across = jnp.sum(jnp.where(r // line == z, spread, 0.0), axis=0, keepdims=True)
    rz = lax.broadcasted_iota(jnp.int32, (rows, lines), 0)
    zz = lax.broadcasted_iota(jnp.int32, (rows, lines), 1)
    picked = jnp.dot((rz // line == zz).astype(BF16), group, preferred_element_type=F32)
    rl = lax.broadcasted_iota(jnp.int32, (rows, line), 0)
    jl = lax.broadcasted_iota(jnp.int32, (rows, line), 1)
    picked = jnp.where(rl % line == jl, picked, 0.0).astype(BF16)
    down = jnp.dot(picked, jnp.ones((line, rows), BF16), preferred_element_type=F32)
    across = across.astype(jnp.int32)
    down = down.astype(jnp.int32)
    sub = lax.broadcasted_iota(jnp.int32, (rows, rows), 0)
    lane = lax.broadcasted_iota(jnp.int32, (rows, rows), 1)
    chip = lax.shift_right_logical(across, 2)
    shared = lax.shift_right_logical(down, 2) == chip
    before = shared & (down * rows + sub < across * rows + lane)
    rank = jnp.sum(jnp.where(before, 1.0, 0.0), axis=0, keepdims=True).astype(jnp.int32)
    number = jnp.sum(jnp.where(shared, 1.0, 0.0), axis=0, keepdims=True).astype(jnp.int32)
    half = lax.shift_right_logical(number + ((lax.axis_index("roll") + chip) & 1), 1)
    core = (rank >= half).astype(jnp.int32)
    device = chip * 2 + core
    place = device * cap + rank - core * half
    place_ref[...] = place
    index = pltpu.make_async_copy(place_ref, where_ref, sems.at[1])
    index.start()
    named = lax.broadcasted_iota(jnp.int32, (4 * owners, rows), 0) == device * 4 + (across & 3)
    counts = jnp.dot(named.astype(BF16), jnp.ones((rows, 128), BF16), preferred_element_type=F32).astype(BF16)
    ii = lax.broadcasted_iota(jnp.int32, (owners * EXTRA, 4 * owners), 0)
    kk = lax.broadcasted_iota(jnp.int32, (owners * EXTRA, 4 * owners), 1)
    repeat = (lax.shift_right_logical(ii, 2) == kk).astype(BF16)
    extra_ref[...] = jnp.dot(repeat, counts, preferred_element_type=F32).astype(BF16).reshape(owners, EXTRA, 128)
    more = pltpu.make_async_copy(extra_ref, out_ref.at[:, pl.ds(cap * per_row, EXTRA), :], sems.at[2])
    more.start()
    index.wait()
    load.wait()

    def one(i, carry):
        at = where_ref[0, i]
        pltpu.make_async_copy(
            held_ref.at[pl.ds(pl.multiple_of(i * per_row, per_row), per_row), :],
            out_ref.at[lax.shift_right_logical(at, 3), pl.ds(pl.multiple_of((at & 7) * per_row, per_row), per_row), :],
            sems.at[0],
        ).start()
        return carry

    lax.fori_loop(0, rows, one, 0, unroll=16)
    more.wait()
    load.wait()


def tail_kernel(steps, per_row, batch, scale, code_ref, q_ref, tk_ref, tv_ref, nk_ref, nv_ref, out_ref, lse_ref):
    base = pl.program_id(0) * batch
    line = code_ref.shape[1]
    slots = tk_ref.shape[0] // batch
    heads = per_row // steps
    total_rows = batch * per_row
    q = q_ref[...]
    parts = []
    lane = lax.broadcasted_iota(jnp.int32, (per_row, slots), 1)
    for i in range(batch):
        r = base + i
        length = code_ref[r // line, r % line] & 255
        s = lax.dot_general(
            q[i * per_row:(i + 1) * per_row], tk_ref[i * slots:(i + 1) * slots, :],
            (((1,), (1,)), ((), ())), preferred_element_type=F32,
        )
        parts.append(jnp.where(lane < length, s, -jnp.inf))
    st = jnp.concatenate(parts, axis=0)
    sn = lax.dot_general(q, nk_ref[...], (((1,), (1,)), ((), ())), preferred_element_type=F32)
    row = lax.broadcasted_iota(jnp.int32, sn.shape, 0)
    col = lax.broadcasted_iota(jnp.int32, sn.shape, 1)
    own = (row // per_row) == (col // steps)
    causal = (col % steps) <= ((row % per_row) // heads)
    sn = jnp.where(own & causal, sn, -jnp.inf)
    top = jnp.maximum(jnp.max(st, axis=1, keepdims=True), jnp.max(sn, axis=1, keepdims=True))
    et = jnp.exp2((st - top) * (scale * LOG2E))
    en = jnp.exp2((sn - top) * (scale * LOG2E))
    total = jnp.sum(et, axis=1, keepdims=True) + jnp.sum(en, axis=1, keepdims=True)
    pt = et.astype(BF16)
    summed = jnp.concatenate(
        [
            jnp.dot(pt[i * per_row:(i + 1) * per_row], tv_ref[i * slots:(i + 1) * slots, :], preferred_element_type=F32)
            for i in range(batch)
        ],
        axis=0,
    )
    summed = summed + jnp.dot(en.astype(BF16), nv_ref[...], preferred_element_type=F32)
    out_ref[...] = summed / total
    lse = top * scale + jnp.log(total)
    mask = lane_group_mask(per_row, 128)
    for i in range(batch):
        one = jnp.where(mask, lse[i * per_row:(i + 1) * per_row], 0.0)
        lse_ref[i:i + 1, :] = jnp.sum(one, axis=0, keepdims=True)


def prefix_kernel(
    cap, per_row, pref, scale, x_ref, k_ref, v_ref, ko_ref, vo_ref, out_ref, key_ref, wide_ref, list_ref, lse_ref,
    where_ref, sems
):
    sources = x_ref.shape[0]
    data = cap * per_row
    own_rows = k_ref.shape[0]
    core = lax.axis_index("roll") & 1
    kept = pl.ds(pl.multiple_of(core * own_rows, own_rows), own_rows)
    other = pl.ds(pl.multiple_of((1 - core) * own_rows, own_rows), own_rows)
    loads = [
        pltpu.make_async_copy(ko_ref, key_ref.at[other, :], sems.at[1]),
        pltpu.make_async_copy(vo_ref, wide_ref.at[other, pl.ds(0, 128)], sems.at[2]),
    ]
    for load in loads:
        load.start()
    i = lax.broadcasted_iota(jnp.int32, (sources, sources), 0)
    j = lax.broadcasted_iota(jnp.int32, (sources, sources), 1)
    lower = (j <= i).astype(BF16)
    source = lax.broadcasted_iota(jnp.int32, (sources, 128), 0).astype(F32)
    lane = lax.broadcasted_iota(jnp.int32, (1, 128), 1).astype(F32)
    tiles = [x_ref[s, data:data + EXTRA, :].astype(F32) for s in range(sources)]
    fore = jnp.zeros((sources, 128), F32)
    end = jnp.zeros((1, 128), F32)
    tables = []
    for g in range(4):
        count = jnp.concatenate([tile[4 * g:4 * g + 1, :] for tile in tiles], axis=0)
        ends = jnp.dot(lower, count.astype(BF16), preferred_element_type=F32)
        total = ends[sources - 1:sources, :]
        tables.append((end, total, ends - count, ends, source * cap + fore))
        fore = fore + count
        end = end + jnp.floor((total + 7.0) * 0.125) * 8.0
    lists = []
    for h in range(3):
        p = jnp.minimum(lane + 128.0 * h, end - 1.0)
        entry = jnp.zeros((1, 128), F32)
        for g, (base, total, begins, ends, first) in enumerate(tables):
            at = jnp.maximum(jnp.minimum(p - base, total - 1.0), 0.0)
            mine = (begins <= at) & (at < ends)
            slot = jnp.sum(jnp.where(mine, first + at - begins, 0.0), axis=0, keepdims=True)
            entry = jnp.where((p >= base) & (total > 0.0), slot + 256.0 * g, entry)
        lists.append(entry)
    list_ref[...] = jnp.concatenate(lists + [end] + lists + [end], axis=0).astype(jnp.int32)
    copy = pltpu.make_async_copy(list_ref, where_ref, sems.at[0])
    copy.start()
    key_ref[kept, :] = k_ref[...]
    wide_ref[kept, 0:128] = v_ref[...]
    wide_ref[:, 128:256] = jnp.ones((2 * own_rows, 128), BF16)
    lse_ref[...] = jnp.zeros(lse_ref.shape, F32)
    copy.wait()
    found = where_ref[3, 0]
    for load in loads:
        load.wait()
    mask = lane_group_mask(per_row, 128)
    factor = scale * LOG2E

    def attend(unit, sub, shifted, begin, stop, bounds):
        def one(b, carry):
            row = lax.shift_right_logical(begin + b * unit, 7)
            first = (begin + b * unit) & 127
            entries = [where_ref[row, first + i] for i in range(unit)]
            slots = [e & 255 for e in entries]
            own = [lax.shift_right_logical(s, 3) for s in slots]
            start = [pl.multiple_of((s & 7) * per_row, per_row) for s in slots]
            here = [pl.multiple_of(lax.shift_right_logical(entries[t], 8) * pref, pref) for t in range(0, unit, sub)]
            scores = []
            for t in range(0, unit, sub):
                q = jnp.concatenate([x_ref[own[i], pl.ds(start[i], per_row), :] for i in range(t, t + sub)], axis=0)
                scores.append(
                    lax.dot_general(
                        q, key_ref[pl.ds(here[t // sub], pref), :], (((1,), (1,)), ((), ())), preferred_element_type=F32
                    )
                )
            low, high = carry
            for t in range(0, unit, sub):
                score = scores[t // sub]
                top = jnp.max(score, axis=1, keepdims=True) if shifted else None
                expo = jnp.exp2((score - top if shifted else score) * factor).astype(BF16)
                both = jnp.dot(expo, wide_ref[pl.ds(here[t // sub], pref), :], preferred_element_type=F32)
                total = both[:, 128:256]
                result = (both[:, 0:128] / total).astype(BF16)
                lse = jnp.log(total)
                if shifted:
                    lse = lse + top * scale
                stacked = total.reshape(sub * per_row // 8, 8, 128)
                low = jnp.minimum(low, jnp.min(stacked, axis=0))
                high = jnp.maximum(high, jnp.max(stacked, axis=0))
                for i in range(sub):
                    part = slice(i * per_row, (i + 1) * per_row)
                    out_ref[own[t + i], pl.ds(start[t + i], per_row), :] = result[part]
                    lse_ref[pl.ds(slots[t + i], 1), :] = jnp.sum(
                        jnp.where(mask, lse[part], 0.0), axis=0, keepdims=True
                    )
            return low, high

        return lax.fori_loop(0, lax.shift_right_logical(stop - begin + unit - 1, unit.bit_length() - 1), one, bounds)

    bounds = (jnp.ones((8, 128), F32), jnp.ones((8, 128), F32))
    long = lax.shift_left(lax.shift_right_logical(found, 6), 6)
    most = lax.shift_left(lax.shift_right_logical(found + 8, 5), 5)
    bounds = attend(64, 8, False, 0, long, bounds)
    bounds = attend(32, 8, False, long, most, bounds)
    low, high = attend(16, 8, False, most, found, bounds)
    safe = (jnp.min(low) > 2.0**-70) & (jnp.max(high) < 2.0**100)

    @pl.when(jnp.logical_not(safe))
    def _():
        attend(8, 8, True, 0, found, bounds)

    for s in range(sources):
        full = lse_ref[s * cap:(s + 1) * cap, :]
        high_part = full.astype(BF16).astype(F32)
        rest = full - high_part
        mid_part = rest.astype(BF16).astype(F32)
        low_part = rest - mid_part
        lanes = lax.broadcasted_iota(jnp.int32, full.shape, 1)
        sent = jnp.where(lanes < per_row, high_part, jnp.where(lanes < 2 * per_row, mid_part, low_part))
        out_ref[s, data:data + BACK, :] = sent.astype(BF16)


def merge_kernel(cap, per_row, chunks, place_ref, x_ref, lse_ref, tail_ref, out_ref, sent_ref, weight_ref, done_ref, sems):
    owners = x_ref.shape[0]
    data = cap * per_row
    rows = lse_ref.shape[0]
    batch = rows // chunks
    part = batch * per_row

    def piece(ref, c):
        return ref.at[pl.ds(c * part, part), :]

    stores = [pltpu.make_async_copy(piece(done_ref, c), piece(out_ref, c), sems.at[c]) for c in range(chunks)]
    for o in range(owners):
        sent_ref[o * cap:(o + 1) * cap, :] = x_ref[o, data:data + BACK, :].astype(F32)
    mask = lane_group_mask(per_row, 128)
    lane = lax.broadcasted_iota(jnp.int32, (batch, 128), 1)
    ones = jnp.ones((128, 128), BF16)
    for c in range(chunks):
        places = [place_ref[0, c * batch + i] for i in range(batch)]
        lse = jnp.concatenate([sent_ref[pl.ds(p, 1), :] for p in places], axis=0)
        terms = jnp.where(lane < 3 * per_row, lse, -lse_ref[c * batch:(c + 1) * batch, :])
        ahead = terms
        for k in range(1, 4):
            ahead = ahead + pltpu.roll(terms, k * per_row, 1)
        weight = 1.0 / (1.0 + jnp.exp(-ahead))
        high = weight.astype(BF16).astype(F32)
        rest = weight - high
        mid = rest.astype(BF16).astype(F32)
        low = jnp.where(lane < 3 * per_row, rest - mid, 0.0)
        weight_ref[c * batch:(c + 1) * batch, :] = jnp.where(lane < per_row, high, jnp.where(lane < 2 * per_row, mid, low))
        spread = jnp.concatenate(
            [jnp.where(mask, weight_ref[c * batch + i:c * batch + i + 1, :], 0.0).astype(BF16) for i in range(batch)], axis=0
        )
        weight_p = jnp.dot(spread, ones, preferred_element_type=F32)
        for i in range(batch):
            here = slice(i * per_row, (i + 1) * per_row)
            there = slice(c * part + i * per_row, c * part + (i + 1) * per_row)
            start = pl.multiple_of((places[i] & 7) * per_row, per_row)
            prefix = x_ref[lax.shift_right_logical(places[i], 3), pl.ds(start, per_row), :].astype(F32)
            tail = tail_ref[there, :]
            done_ref[there, :] = (tail + weight_p[here] * (prefix - tail)).astype(BF16)
        stores[c].start()
    for store in stores:
        store.wait()


def vmem():
    return pl.BlockSpec(memory_space=pltpu.VMEM)


def hbm():
    return pl.BlockSpec(memory_space=pltpu.MemorySpace.HBM)


def in_vmem(x):
    return pltpu.with_memory_space_constraint(x, pltpu.VMEM)


def in_hbm(x):
    return pltpu.with_memory_space_constraint(x, pltpu.HBM)


def smem():
    return pl.BlockSpec(memory_space=pltpu.SMEM)


def body(
    queries, new_keys, new_values, tail_keys, tail_values, prefix_keys, prefix_values, route_owner, group_slot, tail_len
):
    rows, steps, heads, width = queries.shape
    owners = lax.axis_size("roll")
    cap = 8
    per_row = steps * heads
    scale = 1.0 / math.sqrt(width)
    slots = tail_keys.shape[2]
    pref = prefix_keys.shape[2]
    groups = prefix_keys.shape[0]
    block = cap * per_row + EXTRA
    code = (route_owner * 2 + group_slot) * 256 + tail_len
    lines = lax.axis_size("tp")
    codes = lax.all_to_all(jnp.broadcast_to(code, (lines, code.shape[1])), "tp", split_axis=0, concat_axis=0, tiled=True)
    flat = queries.reshape(rows * per_row, width)

    def params(grant):
        return pltpu.CompilerParams(vmem_limit_bytes=grant * MIB)

    sent, place = pl.pallas_call(
        functools.partial(pack_kernel, cap, per_row),
        out_shape=(
            pltpu.HBM((owners, block, width), BF16),
            jax.ShapeDtypeStruct((1, rows), jnp.int32),
        ),
        in_specs=[vmem(), hbm()],
        out_specs=(hbm(), vmem()),
        scratch_shapes=[
            pltpu.VMEM((rows * per_row, width), BF16),
            pltpu.VMEM((owners, EXTRA, 128), BF16),
            pltpu.SMEM((1, rows), jnp.int32),
            pltpu.SemaphoreType.DMA((3,)),
        ],
        compiler_params=params(8),
        cost_estimate=pl.CostEstimate(flops=0, bytes_accessed=3 * MIB, transcendentals=0),
        name="pack",
    )(codes, in_hbm(flat))
    arrived = lax.all_to_all(sent, "roll", split_axis=0, concat_axis=0, tiled=True)

    batch = 8
    part = batch * per_row
    tail_out, tail_lse = pl.pallas_call(
        functools.partial(tail_kernel, steps, per_row, batch, scale),
        out_shape=(
            pltpu.VMEM((rows * per_row, width), F32),
            pltpu.VMEM((rows, 128), F32),
        ),
        grid=(rows // batch,),
        in_specs=[
            smem(),
            pl.BlockSpec((part, width), lambda i: (i, 0)),
            pl.BlockSpec((batch * slots, width), lambda i: (i, 0)),
            pl.BlockSpec((batch * slots, width), lambda i: (i, 0)),
            pl.BlockSpec((batch * steps, width), lambda i: (i, 0)),
            pl.BlockSpec((batch * steps, width), lambda i: (i, 0)),
        ],
        out_specs=(
            pl.BlockSpec((part, width), lambda i: (i, 0)),
            pl.BlockSpec((batch, 128), lambda i: (i, 0)),
        ),
        compiler_params=params(16),
        cost_estimate=pl.CostEstimate(
            flops=4 * rows * per_row * slots * width, bytes_accessed=12 * MIB, transcendentals=rows * per_row * slots
        ),
        name="tail",
    )(
        codes, in_hbm(flat), in_hbm(tail_keys.reshape(rows * slots, width)), in_hbm(tail_values.reshape(rows * slots, width)),
        new_keys.reshape(rows * steps, width), new_values.reshape(rows * steps, width),
    )

    keys = prefix_keys.reshape(groups * pref, width)
    values = prefix_values.reshape(groups * pref, width)
    pairs = [(i, i ^ 1) for i in range(owners)]
    keys_other = lax.ppermute(keys, "roll", pairs)
    values_other = lax.ppermute(values, "roll", pairs)
    arrived, tail_out, tail_lse = lax.optimization_barrier((arrived, tail_out, tail_lse))
    answered = pl.pallas_call(
        functools.partial(prefix_kernel, cap, per_row, pref, scale),
        out_shape=pltpu.VMEM((owners, cap * per_row + BACK, width), BF16),
        in_specs=[vmem()] * 3 + [hbm()] * 2,
        out_specs=vmem(),
        scratch_shapes=[
            pltpu.VMEM((2 * groups * pref, width), BF16),
            pltpu.VMEM((2 * groups * pref, 2 * width), BF16),
            pltpu.VMEM((8, 128), jnp.int32),
            pltpu.VMEM((owners * cap, 128), F32),
            pltpu.SMEM((8, 128), jnp.int32),
            pltpu.SemaphoreType.DMA((3,)),
        ],
        compiler_params=params(24),
        cost_estimate=pl.CostEstimate(
            flops=4 * owners * cap * per_row * pref * width, bytes_accessed=6 * MIB,
            transcendentals=owners * cap * per_row * pref,
        ),
        name="prefix",
    )(arrived, in_vmem(keys), in_vmem(values), in_hbm(keys_other), in_hbm(values_other))
    back = lax.all_to_all(answered, "roll", split_axis=0, concat_axis=0, tiled=True)

    chunks = 4
    merged = pl.pallas_call(
        functools.partial(merge_kernel, cap, per_row, chunks),
        out_shape=pltpu.HBM((rows * per_row, width), BF16),
        in_specs=[smem(), vmem(), vmem(), vmem()],
        out_specs=hbm(),
        scratch_shapes=[
            pltpu.VMEM((owners * cap, 128), F32),
            pltpu.VMEM((rows, 128), F32),
            pltpu.VMEM((rows * per_row, width), BF16),
            pltpu.SemaphoreType.DMA((chunks,)),
        ],
        compiler_params=params(12),
        cost_estimate=pl.CostEstimate(flops=0, bytes_accessed=6 * MIB, transcendentals=0),
        name="merge",
    )(place, in_vmem(back), in_vmem(tail_lse), in_vmem(tail_out))
    return merged.reshape(rows, steps, heads, width)


def solution(mesh):
    return jax.shard_map(
        body,
        mesh=mesh,
        in_specs=(
            P("roll", None, "tp", None),
            P("roll", None, "tp", None),
            P("roll", None, "tp", None),
            P("roll", "tp", None, None),
            P("roll", "tp", None, None),
            P("roll", "tp", None, None),
            P("roll", "tp", None, None),
            P("roll", "tp"),
            P("roll", "tp"),
            P("roll", "tp"),
        ),
        out_specs=P("roll", None, "tp", None),
        check_vma=False,
    )
```

```python
import functools
import math

import jax
import jax.numpy as jnp
from jax import lax
from jax.experimental import pallas as pl
from jax.experimental.pallas import tpu as pltpu
from jax.sharding import PartitionSpec as P

LOG2E = math.log2(math.e)
MIB = 1 << 20
F32 = jnp.float32
BF16 = jnp.bfloat16
EXTRA = 8


def lane_group_mask(per_row, width):
    sub = lax.broadcasted_iota(jnp.int32, (per_row, width), 0)
    lane = lax.broadcasted_iota(jnp.int32, (per_row, width), 1)
    return (lane % per_row) == sub


def pack_kernel(cap, per_row, code_ref, q_ref, out_ref, place_ref, held_ref, extra_ref, where_ref, sems):
    lines, line = code_ref.shape
    rows = lines * line
    owners = out_ref.shape[0]
    load = pltpu.make_async_copy(q_ref, held_ref, sems.at[0])
    load.start()
    group = lax.shift_right_logical(code_ref[...], 8).astype(F32).astype(BF16)
    z = lax.broadcasted_iota(jnp.int32, (lines, rows), 0)
    r = lax.broadcasted_iota(jnp.int32, (lines, rows), 1)
    j = lax.broadcasted_iota(jnp.int32, (line, rows), 0)
    rj = lax.broadcasted_iota(jnp.int32, (line, rows), 1)
    spread = jnp.dot(group, (rj % line == j).astype(BF16), preferred_element_type=F32)
    across = jnp.sum(jnp.where(r // line == z, spread, 0.0), axis=0, keepdims=True)
    rz = lax.broadcasted_iota(jnp.int32, (rows, lines), 0)
    zz = lax.broadcasted_iota(jnp.int32, (rows, lines), 1)
    picked = jnp.dot((rz // line == zz).astype(BF16), group, preferred_element_type=F32)
    rl = lax.broadcasted_iota(jnp.int32, (rows, line), 0)
    jl = lax.broadcasted_iota(jnp.int32, (rows, line), 1)
    picked = jnp.where(rl % line == jl, picked, 0.0).astype(BF16)
    down = jnp.dot(picked, jnp.ones((line, rows), BF16), preferred_element_type=F32)
    across = across.astype(jnp.int32)
    down = down.astype(jnp.int32)
    sub = lax.broadcasted_iota(jnp.int32, (rows, rows), 0)
    lane = lax.broadcasted_iota(jnp.int32, (rows, rows), 1)
    chip = lax.shift_right_logical(across, 2)
    shared = lax.shift_right_logical(down, 2) == chip
    before = shared & (down * rows + sub < across * rows + lane)
    rank = jnp.sum(jnp.where(before, 1.0, 0.0), axis=0, keepdims=True).astype(jnp.int32)
    number = jnp.sum(jnp.where(shared, 1.0, 0.0), axis=0, keepdims=True).astype(jnp.int32)
    half = lax.shift_right_logical(number + ((lax.axis_index("roll") + chip) & 1), 1)
    core = (rank >= half).astype(jnp.int32)
    device = chip * 2 + core
    place = device * cap + rank - core * half
    place_ref[...] = place
    index = pltpu.make_async_copy(place_ref, where_ref, sems.at[1])
    index.start()
    named = lax.broadcasted_iota(jnp.int32, (4 * owners, rows), 0) == device * 4 + (across & 3)
    counts = jnp.dot(named.astype(BF16), jnp.ones((rows, 128), BF16), preferred_element_type=F32).astype(BF16)
    ii = lax.broadcasted_iota(jnp.int32, (owners * EXTRA, 4 * owners), 0)
    kk = lax.broadcasted_iota(jnp.int32, (owners * EXTRA, 4 * owners), 1)
    repeat = (lax.shift_right_logical(ii, 1) == kk).astype(BF16)
    extra_ref[...] = jnp.dot(repeat, counts, preferred_element_type=F32).astype(BF16).reshape(owners, EXTRA, 128)
    more = pltpu.make_async_copy(extra_ref, out_ref.at[:, pl.ds(cap * per_row, EXTRA), :], sems.at[2])
    more.start()
    index.wait()
    load.wait()

    def one(i, carry):
        at = where_ref[0, i]
        pltpu.make_async_copy(
            held_ref.at[pl.ds(pl.multiple_of(i * per_row, per_row), per_row), :],
            out_ref.at[lax.shift_right_logical(at, 3), pl.ds(pl.multiple_of((at & 7) * per_row, per_row), per_row), :],
            sems.at[0],
        ).start()
        return carry

    lax.fori_loop(0, rows, one, 0, unroll=16)
    more.wait()
    load.wait()


def tail_kernel(steps, per_row, batch, scale, code_ref, q_ref, tk_ref, tv_ref, nk_ref, nv_ref, out_ref, lse_ref):
    base = pl.program_id(0) * batch
    line = code_ref.shape[1]
    slots = tk_ref.shape[0] // batch
    heads = per_row // steps
    total_rows = batch * per_row
    q = q_ref[...]
    parts = []
    lane = lax.broadcasted_iota(jnp.int32, (per_row, slots), 1)
    for i in range(batch):
        r = base + i
        length = code_ref[r // line, r % line] & 255
        s = lax.dot_general(
            q[i * per_row:(i + 1) * per_row], tk_ref[i * slots:(i + 1) * slots, :],
            (((1,), (1,)), ((), ())), preferred_element_type=F32,
        )
        parts.append(jnp.where(lane < length, s, -jnp.inf))
    st = jnp.concatenate(parts, axis=0)
    sn = lax.dot_general(q, nk_ref[...], (((1,), (1,)), ((), ())), preferred_element_type=F32)
    row = lax.broadcasted_iota(jnp.int32, sn.shape, 0)
    col = lax.broadcasted_iota(jnp.int32, sn.shape, 1)
    own = (row // per_row) == (col // steps)
    causal = (col % steps) <= ((row % per_row) // heads)
    sn = jnp.where(own & causal, sn, -jnp.inf)
    top = jnp.maximum(jnp.max(st, axis=1, keepdims=True), jnp.max(sn, axis=1, keepdims=True))
    et = jnp.exp2((st - top) * (scale * LOG2E))
    en = jnp.exp2((sn - top) * (scale * LOG2E))
    total = jnp.sum(et, axis=1, keepdims=True) + jnp.sum(en, axis=1, keepdims=True)
    pt = et.astype(BF16)
    summed = jnp.concatenate(
        [
            jnp.dot(pt[i * per_row:(i + 1) * per_row], tv_ref[i * slots:(i + 1) * slots, :], preferred_element_type=F32)
            for i in range(batch)
        ],
        axis=0,
    )
    summed = summed + jnp.dot(en.astype(BF16), nv_ref[...], preferred_element_type=F32)
    out_ref[...] = summed / total
    lse = top * scale + jnp.log(total)
    mask = lane_group_mask(per_row, 128)
    for i in range(batch):
        one = jnp.where(mask, lse[i * per_row:(i + 1) * per_row], 0.0)
        lse_ref[i:i + 1, :] = jnp.sum(one, axis=0, keepdims=True)


def prefix_kernel(
    cap, per_row, pref, scale, x_ref, k_ref, v_ref, ko_ref, vo_ref, out_ref, key_ref, wide_ref, list_ref, lse_ref,
    where_ref, sems
):
    sources = x_ref.shape[0]
    data = cap * per_row
    own_rows = k_ref.shape[0]
    core = lax.axis_index("roll") & 1
    kept = pl.ds(pl.multiple_of(core * own_rows, own_rows), own_rows)
    other = pl.ds(pl.multiple_of((1 - core) * own_rows, own_rows), own_rows)
    loads = [
        pltpu.make_async_copy(ko_ref, key_ref.at[other, :], sems.at[1]),
        pltpu.make_async_copy(vo_ref, wide_ref.at[other, pl.ds(0, 128)], sems.at[2]),
    ]
    for load in loads:
        load.start()
    i = lax.broadcasted_iota(jnp.int32, (sources, sources), 0)
    j = lax.broadcasted_iota(jnp.int32, (sources, sources), 1)
    lower = (j <= i).astype(BF16)
    source = lax.broadcasted_iota(jnp.int32, (sources, 128), 0).astype(F32)
    lane = lax.broadcasted_iota(jnp.int32, (1, 128), 1).astype(F32)
    tiles = [x_ref[s, data:data + EXTRA, :].astype(F32) for s in range(sources)]
    fore = jnp.zeros((sources, 128), F32)
    end = jnp.zeros((1, 128), F32)
    tables = []
    for g in range(4):
        count = jnp.concatenate([tile[2 * g:2 * g + 1, :] for tile in tiles], axis=0)
        ends = jnp.dot(lower, count.astype(BF16), preferred_element_type=F32)
        total = ends[sources - 1:sources, :]
        tables.append((end, total, ends - count, ends, source * cap + fore))
        fore = fore + count
        end = end + jnp.floor((total + 7.0) * 0.125) * 8.0
    lists = []
    for h in range(3):
        p = jnp.minimum(lane + 128.0 * h, end - 1.0)
        entry = jnp.zeros((1, 128), F32)
        for g, (base, total, begins, ends, first) in enumerate(tables):
            at = jnp.maximum(jnp.minimum(p - base, total - 1.0), 0.0)
            mine = (begins <= at) & (at < ends)
            slot = jnp.sum(jnp.where(mine, first + at - begins, 0.0), axis=0, keepdims=True)
            entry = jnp.where((p >= base) & (total > 0.0), slot + 256.0 * g, entry)
        lists.append(entry)
    list_ref[...] = jnp.concatenate(lists + [end] + lists + [end], axis=0).astype(jnp.int32)
    copy = pltpu.make_async_copy(list_ref, where_ref, sems.at[0])
    copy.start()
    key_ref[kept, :] = k_ref[...]
    wide_ref[kept, 0:128] = v_ref[...]
    wide_ref[:, 128:256] = jnp.ones((2 * own_rows, 128), BF16)
    lse_ref[...] = jnp.zeros(lse_ref.shape, F32)
    copy.wait()
    found = where_ref[3, 0]
    for load in loads:
        load.wait()
    mask = lane_group_mask(per_row, 128)
    factor = scale * LOG2E

    def attend(unit, sub, shifted, begin, stop, bounds):
        def one(b, carry):
            row = lax.shift_right_logical(begin + b * unit, 7)
            first = (begin + b * unit) & 127
            entries = [where_ref[row, first + i] for i in range(unit)]
            slots = [e & 255 for e in entries]
            own = [lax.shift_right_logical(s, 3) for s in slots]
            start = [pl.multiple_of((s & 7) * per_row, per_row) for s in slots]
            here = [pl.multiple_of(lax.shift_right_logical(entries[t], 8) * pref, pref) for t in range(0, unit, sub)]
            scores = []
            for t in range(0, unit, sub):
                q = jnp.concatenate([x_ref[own[i], pl.ds(start[i], per_row), :] for i in range(t, t + sub)], axis=0)
                scores.append(
                    lax.dot_general(
                        q, key_ref[pl.ds(here[t // sub], pref), :], (((1,), (1,)), ((), ())), preferred_element_type=F32
                    )
                )
            low, high = carry
            for t in range(0, unit, sub):
                score = scores[t // sub]
                top = jnp.max(score, axis=1, keepdims=True) if shifted else None
                expo = jnp.exp2((score - top if shifted else score) * factor).astype(BF16)
                both = jnp.dot(expo, wide_ref[pl.ds(here[t // sub], pref), :], preferred_element_type=F32)
                total = both[:, 128:256]
                result = (both[:, 0:128] / total).astype(BF16)
                lse = jnp.log(total)
                if shifted:
                    lse = lse + top * scale
                stacked = total.reshape(sub * per_row // 8, 8, 128)
                low = jnp.minimum(low, jnp.min(stacked, axis=0))
                high = jnp.maximum(high, jnp.max(stacked, axis=0))
                for i in range(sub):
                    part = slice(i * per_row, (i + 1) * per_row)
                    out_ref[own[t + i], pl.ds(start[t + i], per_row), :] = result[part]
                    lse_ref[pl.ds(slots[t + i], 1), :] = jnp.sum(
                        jnp.where(mask, lse[part], 0.0), axis=0, keepdims=True
                    )
            return low, high

        return lax.fori_loop(0, lax.shift_right_logical(stop - begin + unit - 1, unit.bit_length() - 1), one, bounds)

    bounds = (jnp.ones((8, 128), F32), jnp.ones((8, 128), F32))
    long = lax.shift_left(lax.shift_right_logical(found, 6), 6)
    most = lax.shift_left(lax.shift_right_logical(found + 8, 5), 5)
    longest = lax.shift_left(lax.shift_right_logical(found, 7), 7)
    bounds = attend(128, 8, False, 0, longest, bounds)
    bounds = attend(64, 8, False, longest, long, bounds)
    bounds = attend(32, 8, False, long, most, bounds)
    low, high = attend(16, 8, False, most, found, bounds)
    safe = (jnp.min(low) > 2.0**-70) & (jnp.max(high) < 2.0**100)

    @pl.when(jnp.logical_not(safe))
    def _():
        attend(8, 8, True, 0, found, bounds)

    for s in range(sources):
        full = lse_ref[s * cap:(s + 1) * cap, :]
        high_part = full.astype(BF16).astype(F32)
        rest = full - high_part
        mid_part = rest.astype(BF16).astype(F32)
        low_part = rest - mid_part
        lanes = lax.broadcasted_iota(jnp.int32, full.shape, 1)
        sent = jnp.where(lanes < per_row, high_part, jnp.where(lanes < 2 * per_row, mid_part, low_part))
        out_ref[s, data:data + EXTRA, :] = sent.astype(BF16)


def merge_kernel(cap, per_row, chunks, place_ref, x_ref, lse_ref, tail_ref, out_ref, sent_ref, weight_ref, done_ref, sems):
    owners = x_ref.shape[0]
    data = cap * per_row
    rows = lse_ref.shape[0]
    batch = rows // chunks
    part = batch * per_row

    def piece(ref, c):
        return ref.at[pl.ds(c * part, part), :]

    stores = [pltpu.make_async_copy(piece(done_ref, c), piece(out_ref, c), sems.at[c]) for c in range(chunks)]
    for o in range(owners):
        sent_ref[o * cap:(o + 1) * cap, :] = x_ref[o, data:data + EXTRA, :].astype(F32)[0:cap, :]
    mask = lane_group_mask(per_row, 128)
    lane = lax.broadcasted_iota(jnp.int32, (batch, 128), 1)
    ones = jnp.ones((128, 128), BF16)
    for c in range(chunks):
        places = [place_ref[0, c * batch + i] for i in range(batch)]
        lse = jnp.concatenate([sent_ref[pl.ds(p, 1), :] for p in places], axis=0)
        terms = jnp.where(lane < 3 * per_row, lse, -lse_ref[c * batch:(c + 1) * batch, :])
        ahead = terms
        for k in range(1, 4):
            ahead = ahead + pltpu.roll(terms, k * per_row, 1)
        weight = 1.0 / (1.0 + jnp.exp(-ahead))
        high = weight.astype(BF16).astype(F32)
        rest = weight - high
        mid = rest.astype(BF16).astype(F32)
        low = jnp.where(lane < 3 * per_row, rest - mid, 0.0)
        weight_ref[c * batch:(c + 1) * batch, :] = jnp.where(lane < per_row, high, jnp.where(lane < 2 * per_row, mid, low))
        spread = jnp.concatenate(
            [jnp.where(mask, weight_ref[c * batch + i:c * batch + i + 1, :], 0.0).astype(BF16) for i in range(batch)], axis=0
        )
        weight_p = jnp.dot(spread, ones, preferred_element_type=F32)
        for i in range(batch):
            here = slice(i * per_row, (i + 1) * per_row)
            there = slice(c * part + i * per_row, c * part + (i + 1) * per_row)
            start = pl.multiple_of((places[i] & 7) * per_row, per_row)
            prefix = x_ref[lax.shift_right_logical(places[i], 3), pl.ds(start, per_row), :].astype(F32)
            tail = tail_ref[there, :]
            done_ref[there, :] = (tail + weight_p[here] * (prefix - tail)).astype(BF16)
        stores[c].start()
    for store in stores:
        store.wait()


def vmem():
    return pl.BlockSpec(memory_space=pltpu.VMEM)


def hbm():
    return pl.BlockSpec(memory_space=pltpu.MemorySpace.HBM)


def in_vmem(x):
    return pltpu.with_memory_space_constraint(x, pltpu.VMEM)


def in_hbm(x):
    return pltpu.with_memory_space_constraint(x, pltpu.HBM)


def smem():
    return pl.BlockSpec(memory_space=pltpu.SMEM)


def body(
    queries, new_keys, new_values, tail_keys, tail_values, prefix_keys, prefix_values, route_owner, group_slot, tail_len
):
    rows, steps, heads, width = queries.shape
    owners = lax.axis_size("roll")
    cap = 8
    per_row = steps * heads
    scale = 1.0 / math.sqrt(width)
    slots = tail_keys.shape[2]
    pref = prefix_keys.shape[2]
    groups = prefix_keys.shape[0]
    block = cap * per_row + EXTRA
    code = (route_owner * 2 + group_slot) * 256 + tail_len
    lines = lax.axis_size("tp")
    codes = lax.all_to_all(jnp.broadcast_to(code, (lines, code.shape[1])), "tp", split_axis=0, concat_axis=0, tiled=True)
    flat = queries.reshape(rows * per_row, width)

    def params(grant):
        return pltpu.CompilerParams(vmem_limit_bytes=grant * MIB)

    sent, place = pl.pallas_call(
        functools.partial(pack_kernel, cap, per_row),
        out_shape=(
            pltpu.HBM((owners, block, width), BF16),
            jax.ShapeDtypeStruct((1, rows), jnp.int32),
        ),
        in_specs=[vmem(), hbm()],
        out_specs=(hbm(), vmem()),
        scratch_shapes=[
            pltpu.VMEM((rows * per_row, width), BF16),
            pltpu.VMEM((owners, EXTRA, 128), BF16),
            pltpu.SMEM((1, rows), jnp.int32),
            pltpu.SemaphoreType.DMA((3,)),
        ],
        compiler_params=params(8),
        cost_estimate=pl.CostEstimate(flops=0, bytes_accessed=3 * MIB, transcendentals=0),
        name="pack",
    )(codes, in_hbm(flat))
    arrived = lax.all_to_all(sent, "roll", split_axis=0, concat_axis=0, tiled=True)

    batch = 8
    part = batch * per_row
    tail_out, tail_lse = pl.pallas_call(
        functools.partial(tail_kernel, steps, per_row, batch, scale),
        out_shape=(
            pltpu.VMEM((rows * per_row, width), F32),
            pltpu.VMEM((rows, 128), F32),
        ),
        grid=(rows // batch,),
        in_specs=[
            smem(),
            pl.BlockSpec((part, width), lambda i: (i, 0)),
            pl.BlockSpec((batch * slots, width), lambda i: (i, 0)),
            pl.BlockSpec((batch * slots, width), lambda i: (i, 0)),
            pl.BlockSpec((batch * steps, width), lambda i: (i, 0)),
            pl.BlockSpec((batch * steps, width), lambda i: (i, 0)),
        ],
        out_specs=(
            pl.BlockSpec((part, width), lambda i: (i, 0)),
            pl.BlockSpec((batch, 128), lambda i: (i, 0)),
        ),
        compiler_params=params(16),
        cost_estimate=pl.CostEstimate(
            flops=4 * rows * per_row * slots * width, bytes_accessed=12 * MIB, transcendentals=rows * per_row * slots
        ),
        name="tail",
    )(
        codes, in_hbm(flat), in_hbm(tail_keys.reshape(rows * slots, width)), in_hbm(tail_values.reshape(rows * slots, width)),
        new_keys.reshape(rows * steps, width), new_values.reshape(rows * steps, width),
    )

    keys = prefix_keys.reshape(groups * pref, width)
    values = prefix_values.reshape(groups * pref, width)
    pairs = [(i, i ^ 1) for i in range(owners)]
    keys_other = lax.ppermute(keys, "roll", pairs)
    values_other = lax.ppermute(values, "roll", pairs)
    arrived, tail_out, tail_lse = lax.optimization_barrier((arrived, tail_out, tail_lse))
    answered = pl.pallas_call(
        functools.partial(prefix_kernel, cap, per_row, pref, scale),
        out_shape=pltpu.VMEM((owners, block, width), BF16),
        in_specs=[vmem()] * 3 + [hbm()] * 2,
        out_specs=vmem(),
        scratch_shapes=[
            pltpu.VMEM((2 * groups * pref, width), BF16),
            pltpu.VMEM((2 * groups * pref, 2 * width), BF16),
            pltpu.VMEM((8, 128), jnp.int32),
            pltpu.VMEM((owners * cap, 128), F32),
            pltpu.SMEM((8, 128), jnp.int32),
            pltpu.SemaphoreType.DMA((3,)),
        ],
        compiler_params=params(24),
        cost_estimate=pl.CostEstimate(
            flops=4 * owners * cap * per_row * pref * width, bytes_accessed=6 * MIB,
            transcendentals=owners * cap * per_row * pref,
        ),
        name="prefix",
    )(arrived, in_vmem(keys), in_vmem(values), in_hbm(keys_other), in_hbm(values_other))
    back = lax.all_to_all(answered, "roll", split_axis=0, concat_axis=0, tiled=True)

    chunks = 4
    merged = pl.pallas_call(
        functools.partial(merge_kernel, cap, per_row, chunks),
        out_shape=pltpu.HBM((rows * per_row, width), BF16),
        in_specs=[smem(), vmem(), vmem(), vmem()],
        out_specs=hbm(),
        scratch_shapes=[
            pltpu.VMEM((owners * cap, 128), F32),
            pltpu.VMEM((rows, 128), F32),
            pltpu.VMEM((rows * per_row, width), BF16),
            pltpu.SemaphoreType.DMA((chunks,)),
        ],
        compiler_params=params(12),
        cost_estimate=pl.CostEstimate(flops=0, bytes_accessed=6 * MIB, transcendentals=0),
        name="merge",
    )(place, in_vmem(back), in_vmem(tail_lse), in_vmem(tail_out))
    return merged.reshape(rows, steps, heads, width)


def solution(mesh):
    return jax.shard_map(
        body,
        mesh=mesh,
        in_specs=(
            P("roll", None, "tp", None),
            P("roll", None, "tp", None),
            P("roll", None, "tp", None),
            P("roll", "tp", None, None),
            P("roll", "tp", None, None),
            P("roll", "tp", None, None),
            P("roll", "tp", None, None),
            P("roll", "tp"),
            P("roll", "tp"),
            P("roll", "tp"),
        ),
        out_specs=P("roll", None, "tp", None),
        check_vma=False,
    )
```
